32 devices in a mesh: seq: 16 (over z, y, core), tp: 2 (over x).
Axes of the slice: x: 2, y: 2, z: 4, core: 2. Of those that a mesh axis runs over, the one named last changes fastest.
Arguments:
- queries: bfloat16 [2048, 1024], P('seq'), may hold values from -8 to 8
- key_rows: bfloat16 [2048, 256], P(('seq', 'tp')), may hold values from -4 to 4
- value_rows: bfloat16 [2048, 256], P(('seq', 'tp')), may hold values from -6 to 6
- ssm_input: bfloat16 [2048, 3072], P('seq', 'tp'), may hold values from -0.29882812 to 0.29882812
- gate_input: bfloat16 [2048, 3072], P('seq', 'tp'), may hold values from -6 to 6
- write_vectors: bfloat16 [2048, 256], P('seq'), may hold values from -1.5 to 1.5
- read_vectors: bfloat16 [2048, 256], P('seq'), may hold values from -1.5 to 1.5
- decay_rates: float32 [2048, 48], P('seq', 'tp'), may hold values from 0 to 3, as said below
- attn_out_weight: bfloat16 [1024, 2048], P('tp'), may hold values from -0.8984375 to 0.8984375
- ssm_out_weight: bfloat16 [3072, 2048], P('tp'), may hold values from -0.109375 to 0.109375
Outputs:
- mixer_output: float32 [2048, 2048], P(('seq', 'tp'))
The draws below stay inside these ranges and needn't reach their ends.
Inputs may be any that keep to these rules, and one draw needn't show every extreme that they name: `decay_rates`: positive.
All inputs are finite; a program needn't handle non-finite values.
Results may differ from the reference program's by a relative error of at most 0.0045.
Values may be sent and summed in bfloat16 or wider, within the bound.
A program may use at most 128 MiB of HBM per device.

```python
import math
import jax
import jax.numpy as jnp
from jax import lax

D = 2048
HEADS = 48
HDIM = 64
STATE = 256
ASKER_PROBES = 8
KVHEADS = 2
HEAD = 128
TOK_DEV = 128
TOKENS = 2048


def shared_signs(key):
    picked = jax.random.uniform(jax.random.fold_in(key, 4401), (KVHEADS, HEAD))
    return jnp.where(picked < 0.5, -1.0, 1.0).astype(jnp.float32)


def draw_queries(key, part):
    inner_key = jax.random.fold_in(key, 17)
    shape = (TOKENS, ASKER_PROBES * HEAD)
    bulk = 2.5 * jax.random.truncated_normal(inner_key, -3.2, 3.2, shape, jnp.float32)
    pattern = jnp.repeat(shared_signs(key), ASKER_PROBES // KVHEADS, axis=0).reshape(-1)
    location_indices = jnp.array([TOKENS // 4 + 3, TOKENS // 2 + 5, 3 * TOKENS // 4 + 7, TOKENS - 1], jnp.int32)
    levels = jnp.array([4.5, 6.0, 7.0, 8.0], jnp.float32)
    similarity_logits = jnp.arange(TOKENS, dtype=jnp.int32)[:, None] == location_indices[None, :]
    strength = jnp.max(jnp.where(similarity_logits, levels[None, :], 0.0), axis=1)
    chosen = jnp.any(similarity_logits, axis=1)
    bulk = jnp.where(chosen[:, None], strength[:, None] * pattern[None, :], bulk)
    return bulk.astype(jnp.bfloat16)


def draw_key_rows(key, part):
    inner_key = jax.random.fold_in(key, 23)
    shape = (TOKENS, KVHEADS * HEAD)
    bulk = jax.random.truncated_normal(inner_key, -4.0, 4.0, shape, jnp.float32)
    pattern = shared_signs(key).reshape(-1)
    row_ids = jnp.arange(TOKENS, dtype=jnp.int32)[:, None]
    bulk = jnp.where(row_ids == 1, 4.0 * pattern[None, :], bulk)
    bulk = jnp.where(row_ids == 2, 3.96875 * pattern[None, :], bulk)
    return bulk.astype(jnp.bfloat16)


def draw_decay_rates(key, part):
    portion_lookup_vectors = jax.random.split(jax.random.fold_in(key, 31), 7)
    fast_share = 0.5
    fast = jax.random.uniform(portion_lookup_vectors[0], (HEADS,)) < fast_share
    fast_rate = jnp.exp(jax.random.uniform(portion_lookup_vectors[1], (HEADS,), jnp.float32, jnp.log(1.0 / 50.0), jnp.log(1.0 / 25.0)))
    slower_decay_rate = 0.3 * jnp.log(10.0) / TOKENS * jnp.exp(jax.random.uniform(portion_lookup_vectors[2], (HEADS,), jnp.float32, -0.69, 0.69))
    head_rate = jnp.where(fast, fast_rate, slower_decay_rate)
    block_factor = jnp.exp(jax.random.uniform(portion_lookup_vectors[3], (TOKENS // TOK_DEV, HEADS), jnp.float32, -0.69, 0.69))
    spread = jnp.repeat(block_factor, TOK_DEV, axis=0)
    rough = jax.random.uniform(portion_lookup_vectors[4], (TOKENS, HEADS), jnp.float32, 0.5, 1.5)
    location_indices = jax.random.randint(portion_lookup_vectors[5], (3,), 0, TOKENS)
    prompt_portions = jax.random.uniform(portion_lookup_vectors[6], (3,), jnp.float32, 0.22, 0.69)
    similarity_logits = jnp.arange(TOKENS, dtype=jnp.int32)[:, None] == location_indices[None, :]
    recurrence_transitions = jnp.sum(jnp.where(similarity_logits, prompt_portions[None, :], 0.0), axis=1)
    return head_rate[None, :] * spread * rough + recurrence_transitions[:, None]


def shard_levels(key, shape, cuts, least, largest):
    loudness, own = 1.0, jax.random.fold_in(key, 6)
    for dim, parts in cuts:
        draws = jnp.exp(jax.random.uniform(jax.random.fold_in(own, dim), (parts,), jnp.float32, least / len(cuts), largest / len(cuts)))
        loudness = loudness * jnp.repeat(draws, shape[dim] // parts).reshape([-1 if axis == dim else 1 for axis in range(len(shape))])
    return loudness


def bell_draw(own_key, shape, scale, most, cuts=(), kind=jnp.bfloat16):
    entries = jax.random.normal(own_key, shape, jnp.float32) * scale
    if len(cuts) > 0:
        entries = shard_levels(own_key, shape, cuts, -0.22, 0.18) * entries
    return jnp.clip(entries, min=-most, max=most).astype(kind)


def setup_inputs(seed: int = 0) -> dict:
    key_list = jax.random.split(jax.random.key(seed), 11)
    queries = draw_queries(jax.random.fold_in(key_list[10], 71), 0)
    key_rows = draw_key_rows(jax.random.fold_in(key_list[10], 71), 0)
    value_rows = bell_draw(key_list[2], (TOKENS, KVHEADS * HEAD), 1.0, 6.0, ((0, 32),))
    ssm_input = bell_draw(key_list[3], (TOKENS, HEADS * HDIM), 0.05, 0.29882812, ((0, 16), (1, 2)))
    gate_input = bell_draw(key_list[4], (TOKENS, HEADS * HDIM), 1.0, 6.0, ((0, 16), (1, 2)))
    write_vectors = bell_draw(key_list[5], (TOKENS, STATE), 0.25, 1.5, ((0, 16),))
    read_vectors = bell_draw(key_list[6], (TOKENS, STATE), 0.25, 1.5, ((0, 16),))
    decay_rates = draw_decay_rates(jax.random.fold_in(key_list[10], 71), 0)
    attn_out_weight = bell_draw(key_list[8], (ASKER_PROBES * HEAD, D), 0.15, 0.8984375, ((0, 2),))
    ssm_out_weight = bell_draw(key_list[9], (HEADS * HDIM, D), (HEADS * HDIM) ** -0.5, 0.109375, ((0, 2),))
    return {"queries": queries, "key_rows": key_rows, "value_rows": value_rows, "ssm_input": ssm_input, "gate_input": gate_input, "write_vectors": write_vectors, "read_vectors": read_vectors, "decay_rates": decay_rates, "attn_out_weight": attn_out_weight, "ssm_out_weight": ssm_out_weight}


precise = lax.Precision.HIGHEST

def ssm_block(carried_state, pieces):
    values_f32, write_f32, read_f32, rates = pieces
    block_rows = values_f32.shape[0]
    decay_sum = jnp.cumsum(-rates, axis=0)
    block_decay = decay_sum[-1]
    positions = jnp.arange(block_rows)
    causal = (positions[:, None] >= positions[None, :])[:, :, None]
    decay_gap = jnp.where(causal, decay_sum[:, None, :] - decay_sum[None, :, :], 0.0)
    decays = jnp.where(causal, jnp.exp(decay_gap), 0.0)
    read_write = jnp.dot(read_f32, write_f32.T, precision=precise)
    within = jnp.einsum('tsh,ts,shp->thp', decays, read_write, values_f32, precision=precise)
    from_before = jnp.einsum('th,tn,hpn->thp', jnp.exp(decay_sum), read_f32, carried_state, precision=precise)
    block_state = jnp.einsum('sh,shp,sn->hpn', jnp.exp(block_decay[None, :] - decay_sum), values_f32, write_f32, precision=precise)
    next_state = jnp.exp(block_decay)[:, None, None] * carried_state + block_state
    return (next_state, within + from_before)

def reference(queries, key_rows, value_rows, ssm_input, gate_input, write_vectors, read_vectors, decay_rates, attn_out_weight, ssm_out_weight):
    blocks = TOKENS // TOK_DEV
    values_f32 = ssm_input.astype(jnp.float32).reshape(blocks, TOK_DEV, HEADS, HDIM)
    write_f32 = write_vectors.astype(jnp.float32).reshape(blocks, TOK_DEV, STATE)
    read_f32 = read_vectors.astype(jnp.float32).reshape(blocks, TOK_DEV, STATE)
    rates = decay_rates.reshape(blocks, TOK_DEV, HEADS)
    initial = jnp.zeros((HEADS, HDIM, STATE), jnp.float32)
    _, ssm_raw = lax.scan(ssm_block, initial, (values_f32, write_f32, read_f32, rates))
    ssm_raw = ssm_raw.reshape(TOKENS, HEADS * HDIM)
    ssm_out = (ssm_raw * jax.nn.silu(gate_input.astype(jnp.float32))).astype(jnp.bfloat16)
    group = ASKER_PROBES // KVHEADS
    query_all = queries.astype(jnp.float32).reshape(TOKENS, KVHEADS, group, HEAD)
    key_all = key_rows.astype(jnp.float32).reshape(TOKENS, KVHEADS, HEAD)
    value_all = value_rows.astype(jnp.float32).reshape(TOKENS, KVHEADS, HEAD)
    block_width = min(256, TOKENS)
    key_place = jnp.arange(TOKENS)
    score_scale = 1.0 / math.sqrt(HEAD)

    def attend(index):
        first_row = (index * block_width).astype(jnp.int32)
        query_tile_rows = lax.dynamic_slice_in_dim(query_all, first_row, block_width, 0)
        scores = jnp.einsum('tgqd,sgd->tgqs', query_tile_rows, key_all, precision=precise) * score_scale
        query_place = first_row + jnp.arange(block_width)
        visible = (key_place[None, :] <= query_place[:, None])[:, None, None, :]
        scores = jnp.where(visible, scores, -1e+30)
        row_max = lax.optimization_barrier(jnp.max(scores, axis=-1, keepdims=True))
        weights = jnp.where(visible, jnp.exp(scores - row_max), 0.0)
        denominator = lax.optimization_barrier(jnp.sum(weights, axis=-1))
        weights_half = lax.optimization_barrier(weights.astype(jnp.bfloat16))
        numerator = jnp.einsum('tgqs,sgd->tgqd', weights_half.astype(jnp.float32), value_all, precision=precise)
        return (numerator / denominator[..., None]).astype(jnp.bfloat16)
    attn = lax.map(attend, jnp.arange(TOKENS // block_width, dtype=jnp.int32))
    attn = attn.reshape(TOKENS, ASKER_PROBES * HEAD)
    summed = jnp.dot(attn, attn_out_weight, preferred_element_type=jnp.float32)
    summed = summed + jnp.dot(ssm_out, ssm_out_weight, preferred_element_type=jnp.float32)
    return summed
```

```python
import functools
import math

import jax
import jax.numpy as jnp
from jax import lax
from jax.experimental import pallas as pl
from jax.experimental.pallas import tpu as pltpu
from jax.sharding import PartitionSpec as P

KVHEADS = 2
HEAD = 128
HDIM = 64
PLANE = 4
MESH = pl.DeviceIdType.MESH
F32 = jnp.float32
BF16 = jnp.bfloat16
PRECISE = lax.Precision.HIGHEST


def dot(a, b):
    return jnp.dot(a, b, preferred_element_type=F32)


def dot_tn(a, b, precision=None):
    dims = (((0,), (0,)), ((), ()))
    return lax.dot_general(a, b, dims, precision=precision, preferred_element_type=F32)


def dot_nt(a, b):
    dims = (((1,), (1,)), ((), ()))
    return lax.dot_general(a, b, dims, preferred_element_type=F32)


def quarter_starts(width):
    span = -(-width // (PLANE * 128)) * 128
    return span, [min(q * span, width - span) for q in range(PLANE)]


def kernel(
    n, tp, heads, nq,
    q_ref, k_ref, v_ref, x_ref, gate_ref, b_ref, c_ref, rate_ref, wa_hbm, ws_hbm,
    out_ref,
    wa, ws, kv, bc, xs, xr, ds, dr, loc, tot, er, es, ysend, yrecv, psend, precv,
    qs, attn, yacc, grow, part, ssm, acc, peak, norm,
    wsem, swap_s, swap_r, col_s, col_r, pl_s, pl_r, bc_s, bc_r, x_s, x_r, d_s, d_r,
    e_s, e_r, y_s, y_r, p_s, p_r,
):
    s = lax.axis_index("seq")
    t = lax.axis_index("tp")
    planes = n // PLANE
    z = s // PLANE
    i = s % PLANE
    rows = q_ref.shape[0]
    width = x_ref.shape[1]
    model = wa.shape[1]
    own = rows // tp
    span, starts = quarter_starts(width)
    nch = span // 128
    ncol = psend.shape[0]
    cols = model // ncol

    def copy(src, dst, send, recv, to):
        return pltpu.make_async_remote_copy(
            src_ref=src, dst_ref=dst, send_sem=send, recv_sem=recv,
            device_id=to, device_id_type=MESH,
        )

    w_copies = [
        pltpu.make_async_copy(wa_hbm, wa, wsem.at[0]),
        pltpu.make_async_copy(ws_hbm, ws, wsem.at[1]),
    ]
    for w in w_copies:
        w.start()

    plane_peers = [z * PLANE + (i + d) % PLANE for d in range(1, PLANE)]
    plane_index = [(i + d) % PLANE for d in range(1, PLANE)]
    tp_peers = [(t + d) % tp for d in range(1, tp)]
    col_peers = [((z + d) % planes) * PLANE + i for d in range(1, planes)]

    barrier = pltpu.get_barrier_semaphore()
    for p in plane_peers + col_peers:
        pl.semaphore_signal(barrier, inc=1, device_id=(p, t), device_id_type=MESH)
    for p in tp_peers:
        pl.semaphore_signal(barrier, inc=1, device_id=(s, p), device_id_type=MESH)
    pl.semaphore_wait(barrier, len(plane_peers) + len(col_peers) + len(tp_peers))

    def kv_cols(peer):
        return pl.ds(pl.multiple_of(peer * KVHEADS // tp * HEAD, HEAD), HEAD)

    def own_rows(peer):
        return pl.ds(pl.multiple_of(peer * own, own), own)

    swaps = []
    for d, p in enumerate(tp_peers):
        for m, ref in enumerate((k_ref, v_ref)):
            swaps.append(copy(
                ref.at[:, kv_cols(p)], kv.at[s, m, own_rows(t)],
                swap_s.at[m, d], swap_r.at[m, d], (s, p),
            ))
    for c in swaps:
        c.start()
    for m, ref in enumerate((k_ref, v_ref)):
        kv[s, m, own_rows(t), :] = ref[:, kv_cols(t)]

    bc_copies = []
    for d, p in enumerate(plane_peers):
        for m, ref in enumerate((b_ref, c_ref)):
            bc_copies.append(copy(
                ref, bc.at[i, m], bc_s.at[m, d], bc_r.at[m, d], (p, t)
            ))
    for c in bc_copies:
        c.start()
    bc[i, 0] = b_ref[...]
    bc[i, 1] = c_ref[...]

    row_id = lax.broadcasted_iota(jnp.int32, (rows, rows), 0)
    col_id = lax.broadcasted_iota(jnp.int32, (rows, rows), 1)
    causal = row_id >= col_id
    lower = jnp.where(causal, 1.0, 0.0).astype(F32)
    upper = jnp.where(row_id <= col_id, 1.0, 0.0).astype(F32)
    rates = -rate_ref[...]
    cum = jnp.dot(lower, rates, precision=PRECISE, preferred_element_type=F32)
    cum_t = dot_tn(rates, upper, PRECISE)
    last = cum[rows - 1:rows, :]
    to_end = jnp.exp(last - cum)
    from_start = jnp.exp(cum)
    whole_decay = jnp.exp(last)
    first_half = lax.broadcasted_iota(jnp.int32, (rows, 128), 1) < HDIM
    first_half_8 = lax.broadcasted_iota(jnp.int32, (8, 128), 1) < HDIM

    def pair_cols(value, pair):
        a = value[:, 2 * pair:2 * pair + 1]
        b = value[:, 2 * pair + 1:2 * pair + 2]
        mask = first_half if value.shape[0] == rows else first_half_8
        return jnp.where(mask, a, b)

    for q in range(PLANE):
        for c in range(nch):
            lo = starts[q] + 128 * c
            pair = lo // 128
            x = x_ref[:, lo:lo + 128].astype(F32)
            xs[q, :, 128 * c:128 * (c + 1)] = (x * pair_cols(to_end, pair)).astype(BF16)
            ds[q, :, 128 * c:128 * (c + 1)] = pair_cols(whole_decay, pair)

    x_copies = []
    for d, p in enumerate(plane_peers):
        x_copies.append(copy(
            xs.at[plane_index[d]], xr.at[i], x_s.at[d], x_r.at[d], (p, t)
        ))
        x_copies.append(copy(
            ds.at[plane_index[d]], dr.at[i], d_s.at[d], d_r.at[d], (p, t)
        ))
    for c in x_copies:
        c.start()
    xr[i] = xs[i]
    dr[i] = ds[i]

    for c in swaps:
        c.wait_recv()

    def to_plane(block):
        src = kv.at[block * PLANE + i]
        return [
            copy(src, src, pl_s.at[block, d], pl_r.at[block, d], (p, t))
            for d, p in enumerate(plane_peers)
        ]

    def up(zz):
        src = kv.at[s]
        return copy(src, src, col_s.at[zz], col_r.at[z], (zz * PLANE + i, t))

    def col_from(zz):
        src = kv.at[zz * PLANE + i]
        return copy(src, src, col_s.at[zz], col_r.at[zz], (s, t))

    @pl.loop(z + 1, planes)
    def _(zz):
        up(zz).start()

    for c in to_plane(z):
        c.start()

    read_write = dot_nt(c_ref[...], b_ref[...])
    for pair in range(width // 128):
        cc = slice(128 * pair, 128 * (pair + 1))
        factors = []
        for h in (2 * pair, 2 * pair + 1):
            gap = jnp.minimum(cum[:, h:h + 1] - cum_t[h:h + 1, :], 0.0)
            factors.append(jnp.where(causal, jnp.exp(gap) * read_write, 0.0).astype(BF16))
        x = x_ref[:, cc]
        zero = jnp.zeros_like(x)
        stacked = jnp.concatenate(
            [jnp.where(first_half, x, zero), jnp.where(first_half, zero, x)], axis=0
        )
        yacc[:, cc] = dot(jnp.concatenate(factors, axis=1), stacked)
        grow[:, cc] = pair_cols(from_start, pair)

    for c in bc_copies + x_copies:
        c.wait_recv()
    for c in range(nch):
        cc = slice(128 * c, 128 * (c + 1))
        total = jnp.zeros((bc.shape[3], 128), F32)
        decay = jnp.ones((1, 128), F32)
        for j in range(PLANE):
            block = dot_tn(bc[j, 0], xr[j, :, cc])
            loc[j, :, cc] = block
            total = dr[j, 0:1, cc] * total + block
            decay = decay * dr[j, 0:1, cc]
        tot[0, :, cc] = total
        dr[PLANE, :, cc] = jnp.broadcast_to(decay, (8, 128))

    def chain(c):
        to = (jnp.minimum(z + 1, planes - 1) * PLANE + i, t)
        return copy(es.at[c], er.at[c], e_s.at[c], e_r.at[c], to)

    @pl.when(z == 0)
    def _():
        er[...] = jnp.zeros_like(er)

    @pl.loop(0, z)
    def _(zz):
        col_from(zz).wait_recv()
        for c in to_plane(zz):
            c.start()

    for c in range(nch):
        cc = slice(128 * c, 128 * (c + 1))

        @pl.when(z > 0)
        def _():
            chain(c).wait_recv()

        @pl.when(z < planes - 1)
        def _():
            entering = er[c].astype(F32)
            es[c] = (dr[PLANE, 0:1, cc] * entering + tot[0, :, cc]).astype(BF16)
            chain(c).start()

    for c in range(nch):
        cc = slice(128 * c, 128 * (c + 1))
        state = er[c].astype(F32)
        for j in range(PLANE):
            ysend[j, :, cc] = dot(bc[j, 1], state.astype(BF16)).astype(BF16)
            if j < PLANE - 1:
                state = dr[j, 0:1, cc] * state + loc[j, :, cc]
    y_copies = [
        copy(ysend.at[plane_index[d]], yrecv.at[i], y_s.at[d], y_r.at[d], (p, t))
        for d, p in enumerate(plane_peers)
    ]
    for c in y_copies:
        c.start()
    yrecv[i] = ysend[i]

    for h in range(nq):
        lo = pl.multiple_of((t * nq + h) * HEAD, HEAD)
        qs[h * rows:(h + 1) * rows, :] = q_ref[:, pl.ds(lo, HEAD)]
    stack = nq * rows
    acc[...] = jnp.zeros_like(acc)
    norm[...] = jnp.zeros_like(norm)
    peak[...] = jnp.full_like(peak, -1e30)
    scale = 1.0 / math.sqrt(HEAD)
    wide = PLANE * rows

    def attend(zz, masked):
        for c in to_plane(zz):
            c.wait_recv()
        keys = kv[pl.ds(zz * PLANE, PLANE), 0].reshape(wide, HEAD)
        vals = kv[pl.ds(zz * PLANE, PLANE), 1].reshape(wide, HEAD)
        for h in range(nq):
            hh = slice(h * rows, (h + 1) * rows)
            scores = dot_nt(qs[hh, :], keys) * scale
            if masked:
                key_id = lax.broadcasted_iota(jnp.int32, (rows, wide), 1)
                query_id = lax.broadcasted_iota(jnp.int32, (rows, wide), 0) + i * rows
                scores = jnp.where(key_id <= query_id, scores, -1e30)
            old = peak[hh, 0:1]
            new = jnp.maximum(old, jnp.max(scores, axis=1, keepdims=True))
            weights = jnp.exp(scores - new)
            shrink = jnp.exp(old - new)
            norm[hh, 0:1] = norm[hh, 0:1] * shrink + jnp.sum(weights, axis=1, keepdims=True)
            acc[hh, :] = acc[hh, :] * shrink + dot(weights.astype(BF16), vals)
            peak[hh, 0:1] = new

    attend(z, True)

    @pl.loop(0, z)
    def _(zz):
        attend(zz, False)

    for h in range(nq):
        hh = slice(h * rows, (h + 1) * rows)
        attn[:, h * HEAD:(h + 1) * HEAD] = (acc[hh, :] / norm[hh, 0:1]).astype(BF16)
    for w in w_copies:
        w.wait()
    for k in range(ncol):
        cc = slice(k * cols, (k + 1) * cols)
        part[:, cc] = dot(attn[...], wa[:, cc])

    for c in y_copies:
        c.wait_recv()
    for q in range(PLANE):
        for c in range(nch):
            lo = starts[q] + 128 * c
            cc = slice(lo, lo + 128)
            g = gate_ref[:, cc].astype(F32)
            raw = yacc[:, cc] + grow[:, cc] * yrecv[q, :, 128 * c:128 * (c + 1)].astype(F32)
            ssm[:, cc] = (raw * (g / (1.0 + jnp.exp(-g)))).astype(BF16)
    p_copies = []
    for k in range(ncol):
        cc = slice(k * cols, (k + 1) * cols)
        value = part[:, cc] + dot(ssm[...], ws[:, cc])
        part[:, cc] = value
        psend[k] = value.astype(BF16)
        for d, p in enumerate(tp_peers):
            c = copy(
                psend.at[k, own_rows(p)], precv.at[d, k],
                p_s.at[d, k], p_r.at[d, k], (s, p),
            )
            c.start()
            p_copies.append((d, k, c))
    for k in range(ncol):
        cc = slice(k * cols, (k + 1) * cols)
        value = part[own_rows(t), cc]
        for d, kk, c in p_copies:
            if kk == k:
                c.wait_recv()
                value = value + precv[d, k].astype(F32)
        out_ref[:, cc] = value

    for c in swaps + bc_copies + x_copies + y_copies + [c for _, _, c in p_copies]:
        c.wait_send()

    @pl.loop(z + 1, planes)
    def _(zz):
        up(zz).wait_send()

    @pl.loop(0, z + 1)
    def _(zz):
        for c in to_plane(zz):
            c.wait_send()

    @pl.when(z < planes - 1)
    def _():
        for c in range(nch):
            chain(c).wait_send()


def local(
    n, tp,
    queries, key_rows, value_rows, ssm_input, gate_input, write_vectors, read_vectors,
    decay_rates, attn_out_weight, ssm_out_weight,
):
    rows = queries.shape[0]
    width = ssm_input.shape[1]
    heads = decay_rates.shape[1]
    state = write_vectors.shape[1]
    model = attn_out_weight.shape[1]
    nq = queries.shape[1] // HEAD // tp
    planes = n // PLANE
    own = rows // tp
    span, _ = quarter_starts(width)
    nch = span // 128
    ncol = 4
    cols = model // ncol
    peers = PLANE - 1
    vmem = pltpu.VMEM
    dma = pltpu.SemaphoreType.DMA
    return pl.pallas_call(
        functools.partial(kernel, n, tp, heads, nq),
        out_shape=jax.ShapeDtypeStruct((own, model), F32),
        in_specs=[pl.BlockSpec(memory_space=pltpu.VMEM)] * 8
        + [pl.BlockSpec(memory_space=pl.ANY)] * 2,
        out_specs=pl.BlockSpec(memory_space=pltpu.VMEM),
        scratch_shapes=[
            vmem(attn_out_weight.shape, BF16),
            vmem(ssm_out_weight.shape, BF16),
            vmem((n, 2, rows, HEAD), BF16),
            vmem((PLANE, 2, rows, state), BF16),
            vmem((PLANE, rows, span), BF16),
            vmem((PLANE, rows, span), BF16),
            vmem((PLANE, 8, span), F32),
            vmem((PLANE + 1, 8, span), F32),
            vmem((PLANE, state, span), F32),
            vmem((1, state, span), F32),
            vmem((nch, state, 128), BF16),
            vmem((nch, state, 128), BF16),
            vmem((PLANE, rows, span), BF16),
            vmem((PLANE, rows, span), BF16),
            vmem((ncol, rows, cols), BF16),
            vmem((tp - 1, ncol, own, cols), BF16),
            vmem((nq * rows, HEAD), BF16),
            vmem((rows, nq * HEAD), BF16),
            vmem((rows, width), F32),
            vmem((rows, width), F32),
            vmem((rows, model), F32),
            vmem((rows, width), BF16),
            vmem((nq * rows, HEAD), F32),
            vmem((nq * rows, HEAD), F32),
            vmem((nq * rows, HEAD), F32),
            dma((2,)),
            dma((2, tp - 1)),
            dma((2, tp - 1)),
            dma((planes,)),
            dma((planes,)),
            dma((planes, peers)),
            dma((planes, peers)),
            dma((2, peers)),
            dma((2, peers)),
            dma((peers,)),
            dma((peers,)),
            dma((peers,)),
            dma((peers,)),
            dma((nch,)),
            dma((nch,)),
            dma((peers,)),
            dma((peers,)),
            dma((tp - 1, ncol)),
            dma((tp - 1, ncol)),
        ],
        compiler_params=pltpu.CompilerParams(
            collective_id=0, has_side_effects=True, vmem_limit_bytes=56 * 1024 * 1024
        ),
    )(
        queries, key_rows, value_rows, ssm_input, gate_input, write_vectors, read_vectors,
        decay_rates, attn_out_weight, ssm_out_weight,
    )


def solution(mesh):
    placed = (
        P("seq", None),
        P(("seq", "tp"), None),
        P(("seq", "tp"), None),
        P("seq", "tp"),
        P("seq", "tp"),
        P("seq", None),
        P("seq", None),
        P("seq", "tp"),
        P("tp", None),
        P("tp", None),
    )
    body = functools.partial(local, mesh.shape["seq"], mesh.shape["tp"])
    return jax.shard_map(
        body, mesh=mesh, in_specs=placed, out_specs=P(("seq", "tp"), None), check_vma=False
    )
```

```python
import functools
import math

import jax
import jax.numpy as jnp
from jax import lax
from jax.experimental import pallas as pl
from jax.experimental.pallas import tpu as pltpu
from jax.sharding import PartitionSpec as P

KVHEADS = 2
HEAD = 128
HDIM = 64
PLANE = 4
MESH = pl.DeviceIdType.MESH
F32 = jnp.float32
BF16 = jnp.bfloat16
PRECISE = lax.Precision.HIGHEST


def dot(a, b):
    return jnp.dot(a, b, preferred_element_type=F32)


def dot_tn(a, b, precision=None):
    dims = (((0,), (0,)), ((), ()))
    return lax.dot_general(a, b, dims, precision=precision, preferred_element_type=F32)


def dot_nt(a, b, precision=None):
    dims = (((1,), (1,)), ((), ()))
    return lax.dot_general(a, b, dims, precision=precision, preferred_element_type=F32)


def quarter_starts(width):
    span = -(-width // (PLANE * 128)) * 128
    return span, [min(q * span, width - span) for q in range(PLANE)]


def kernel(
    n, tp, heads, nq,
    q_ref, k_ref, v_ref, x_ref, gate_ref, b_ref, c_ref, rate_ref, wa_hbm, ws_hbm,
    out_ref, precv,
    wa, ws, kv, bc, xs, xr, ds, dr, loc, tot, er, es, ysend, yrecv, psend,
    qs, attn, yacc, grow, part, ssm, acc, peak, norm,
    wsem, swap_s, swap_r, col_s, col_r, pl_s, pl_r, bc_s, bc_r, x_s, x_r, d_s, d_r,
    e_s, e_r, y_s, y_r, p_s, p_r, o_s,
):
    s = lax.axis_index("seq")
    t = lax.axis_index("tp")
    planes = n // PLANE
    z = s // PLANE
    i = s % PLANE
    rows = q_ref.shape[0]
    width = x_ref.shape[1]
    model = wa.shape[1]
    own = rows // tp
    span, starts = quarter_starts(width)
    nch = span // 128
    ncol = psend.shape[0]
    cols = model // ncol

    def copy(src, dst, send, recv, to):
        return pltpu.make_async_remote_copy(
            src_ref=src, dst_ref=dst, send_sem=send, recv_sem=recv,
            device_id=to, device_id_type=MESH,
        )

    w_copies = [
        pltpu.make_async_copy(wa_hbm, wa, wsem.at[0]),
        pltpu.make_async_copy(ws_hbm, ws, wsem.at[1]),
    ]
    for w in w_copies:
        w.start()

    sib = i + 1 - 2 * (i % 2)
    ynb = (i + 2) % PLANE
    dia = (sib + 2) % PLANE
    plane_index = [ynb, dia, sib]
    plane_peers = [z * PLANE + j for j in plane_index]
    tp_peers = [(t + d) % tp for d in range(1, tp)]
    col_peers = [((z + d) % planes) * PLANE + i for d in range(1, planes)]

    barrier = pltpu.get_barrier_semaphore()
    for p in plane_peers + col_peers:
        pl.semaphore_signal(barrier, inc=1, device_id=(p, t), device_id_type=MESH)
    for p in tp_peers:
        pl.semaphore_signal(barrier, inc=1, device_id=(s, p), device_id_type=MESH)
    pl.semaphore_wait(barrier, len(plane_peers) + len(col_peers) + len(tp_peers))

    def kv_cols(peer):
        return pl.ds(pl.multiple_of(peer * KVHEADS // tp * HEAD, HEAD), HEAD)

    def own_rows(peer):
        return pl.ds(pl.multiple_of(peer * own, own), own)

    swaps = []
    for d, p in enumerate(tp_peers):
        for m, ref in enumerate((k_ref, v_ref)):
            swaps.append(copy(
                ref.at[:, kv_cols(p)], kv.at[s, m, own_rows(t)],
                swap_s.at[m, d], swap_r.at[m, d], (s, p),
            ))
    for c in swaps:
        c.start()
    for m, ref in enumerate((k_ref, v_ref)):
        kv[s, m, own_rows(t), :] = ref[:, kv_cols(t)]

    def relay(ref_of, send, recv):
        def move(block, kind, to):
            ref = ref_of(block)
            return copy(ref, ref, send.at[kind], recv.at[kind], (z * PLANE + to, t))
        return [move(i, 0, sib), move(i, 1, ynb), move(ynb, 2, sib)]

    bc[i, 0] = b_ref[...]
    bc[i, 1] = c_ref[...]
    b_moves = relay(lambda j: bc.at[j, 0], bc_s.at[0], bc_r.at[0])
    c_moves = relay(lambda j: bc.at[j, 1], bc_s.at[1], bc_r.at[1])
    b_moves[1].start()
    b_moves[0].start()

    row_id = lax.broadcasted_iota(jnp.int32, (rows, rows), 0)
    col_id = lax.broadcasted_iota(jnp.int32, (rows, rows), 1)
    causal = row_id >= col_id
    lower = jnp.where(causal, 1.0, 0.0).astype(F32)
    upper = jnp.where(row_id <= col_id, 1.0, 0.0).astype(F32)
    rates = -rate_ref[...]
    cum_t = jnp.dot(rates, upper, precision=PRECISE, preferred_element_type=F32)
    cum = dot_nt(lower, rates, PRECISE)
    last = cum[rows - 1:rows, :]
    to_end = jnp.exp(last - cum)
    from_start = jnp.exp(cum)
    whole_decay = jnp.exp(last)
    first_half = lax.broadcasted_iota(jnp.int32, (rows, 128), 1) < HDIM
    first_half_8 = lax.broadcasted_iota(jnp.int32, (8, 128), 1) < HDIM

    def pair_cols(value, pair):
        a = value[:, 2 * pair:2 * pair + 1]
        b = value[:, 2 * pair + 1:2 * pair + 2]
        mask = first_half if value.shape[0] == rows else first_half_8
        return jnp.where(mask, a, b)

    for q in range(PLANE):
        for c in range(nch):
            lo = starts[q] + 128 * c
            pair = lo // 128
            x = x_ref[:, lo:lo + 128].astype(F32)
            xs[q, :, 128 * c:128 * (c + 1)] = (x * pair_cols(to_end, pair)).astype(BF16)
            ds[q, :, 128 * c:128 * (c + 1)] = pair_cols(whole_decay, pair)

    x_copies = []
    for d, p in enumerate(plane_peers):
        x_copies.append(copy(
            xs.at[plane_index[d]], xr.at[i], x_s.at[d], x_r.at[d], (p, t)
        ))
        x_copies.append(copy(
            ds.at[plane_index[d]], dr.at[i], d_s.at[d], d_r.at[d], (p, t)
        ))
    for c in x_copies:
        c.start()
    c_moves[1].start()
    c_moves[0].start()
    b_moves[1].wait_recv()
    b_moves[2].start()
    xr[i] = xs[i]
    dr[i] = ds[i]

    for c in swaps:
        c.wait_recv()

    def kv_moves(zz):
        return relay(lambda j: kv.at[zz * PLANE + j], pl_s.at[zz], pl_r.at[zz])

    def up(zz):
        src = kv.at[s]
        return copy(src, src, col_s.at[zz], col_r.at[z], (zz * PLANE + i, t))

    def col_from(zz):
        src = kv.at[zz * PLANE + i]
        return copy(src, src, col_s.at[zz], col_r.at[zz], (s, t))

    @pl.loop(z + 1, planes)
    def _(zz):
        up(zz).start()

    for c in kv_moves(z)[:2]:
        c.start()

    read_write = dot_nt(c_ref[...], b_ref[...])
    for pair in range(width // 128):
        cc = slice(128 * pair, 128 * (pair + 1))
        factors = []
        for h in (2 * pair, 2 * pair + 1):
            gap = jnp.minimum(cum[:, h:h + 1] - cum_t[h:h + 1, :], 0.0)
            factors.append(jnp.where(causal, jnp.exp(gap) * read_write, 0.0).astype(BF16))
        x = x_ref[:, cc]
        zero = jnp.zeros_like(x)
        stacked = jnp.concatenate(
            [jnp.where(first_half, x, zero), jnp.where(first_half, zero, x)], axis=0
        )
        yacc[:, cc] = dot(jnp.concatenate(factors, axis=1), stacked)
        grow[:, cc] = pair_cols(from_start, pair)

    c_moves[1].wait_recv()
    c_moves[2].start()
    for c in [b_moves[0], b_moves[2]] + x_copies:
        c.wait_recv()
    total = jnp.zeros((bc.shape[3], span), F32)
    decay = jnp.ones((1, span), F32)
    for j in range(PLANE):
        block = dot_tn(bc[j, 0], xr[j])
        loc[j] = block
        total = dr[j, 0:1, :] * total + block
        decay = decay * dr[j, 0:1, :]
    tot[0] = total
    dr[PLANE] = jnp.broadcast_to(decay, (8, span))

    def chain(c):
        to = (jnp.minimum(z + 1, planes - 1) * PLANE + i, t)
        return copy(es.at[c], er.at[c], e_s.at[c], e_r.at[c], to)

    @pl.when(z == 0)
    def _():
        er[...] = jnp.zeros_like(er)

    @pl.loop(0, z)
    def _(zz):
        col_from(zz).wait_recv()
        for c in kv_moves(zz)[:2]:
            c.start()

    @pl.when(z == 0)
    def _():
        for c in range(nch):
            es[c] = tot[0, :, 128 * c:128 * (c + 1)].astype(BF16)
            chain(c).start()

    @pl.loop(0, z + 1)
    def _(zz):
        moves = kv_moves(zz)
        moves[1].wait_recv()
        moves[2].start()

    for h in range(nq):
        lo = pl.multiple_of((t * nq + h) * HEAD, HEAD)
        qs[h * rows:(h + 1) * rows, :] = q_ref[:, pl.ds(lo, HEAD)]
    stack = nq * rows
    acc[...] = jnp.zeros_like(acc)
    norm[...] = jnp.zeros_like(norm)
    peak[...] = jnp.full_like(peak, -1e30)
    scale = 1.0 / math.sqrt(HEAD)
    wide = PLANE * rows

    def attend(zz, masked):
        moves = kv_moves(zz)
        moves[0].wait_recv()
        moves[2].wait_recv()
        keys = kv[pl.ds(zz * PLANE, PLANE), 0].reshape(wide, HEAD)
        vals = kv[pl.ds(zz * PLANE, PLANE), 1].reshape(wide, HEAD)
        for h in range(nq):
            hh = slice(h * rows, (h + 1) * rows)
            scores = dot_nt(qs[hh, :], keys) * scale
            if masked:
                key_id = lax.broadcasted_iota(jnp.int32, (rows, wide), 1)
                query_id = lax.broadcasted_iota(jnp.int32, (rows, wide), 0) + i * rows
                scores = jnp.where(key_id <= query_id, scores, -1e30)
            old = peak[hh, 0:1]
            new = jnp.maximum(old, jnp.max(scores, axis=1, keepdims=True))
            weights = jnp.exp(scores - new)
            shrink = jnp.exp(old - new)
            norm[hh, 0:1] = norm[hh, 0:1] * shrink + jnp.sum(weights, axis=1, keepdims=True)
            acc[hh, :] = acc[hh, :] * shrink + dot(weights.astype(BF16), vals)
            peak[hh, 0:1] = new

    early = z // 2 + (z // (planes - 1)) * (z - z // 2)

    @pl.loop(0, early)
    def _(zz):
        attend(zz, False)

    for c in range(nch):
        cc = slice(128 * c, 128 * (c + 1))

        @pl.when(z > 0)
        def _():
            chain(c).wait_recv()

        @pl.when((z > 0) & (z < planes - 1))
        def _():
            entering = er[c].astype(F32)
            es[c] = (dr[PLANE, 0:1, cc] * entering + tot[0, :, cc]).astype(BF16)
            chain(c).start()

    c_moves[0].wait_recv()
    c_moves[2].wait_recv()
    for c in range(nch):
        cc = slice(128 * c, 128 * (c + 1))
        state = er[c].astype(F32)
        for j in range(PLANE):
            ysend[j, :, cc] = dot(bc[j, 1], state.astype(BF16)).astype(BF16)
            if j < PLANE - 1:
                state = dr[j, 0:1, cc] * state + loc[j, :, cc]
    y_copies = [
        copy(ysend.at[plane_index[d]], yrecv.at[i], y_s.at[d], y_r.at[d], (p, t))
        for d, p in enumerate(plane_peers)
    ]
    for c in y_copies:
        c.start()
    yrecv[i] = ysend[i]

    attend(z, True)

    @pl.loop(early, z)
    def _(zz):
        attend(zz, False)

    for h in range(nq):
        hh = slice(h * rows, (h + 1) * rows)
        attn[:, h * HEAD:(h + 1) * HEAD] = (acc[hh, :] / norm[hh, 0:1]).astype(BF16)
    for w in w_copies:
        w.wait()
    for k in range(ncol):
        cc = slice(k * cols, (k + 1) * cols)
        part[:, cc] = dot(attn[...], wa[:, cc])

    for c in y_copies:
        c.wait_recv()
    for q in range(PLANE):
        for c in range(nch):
            lo = starts[q] + 128 * c
            cc = slice(lo, lo + 128)
            g = gate_ref[:, cc].astype(F32)
            raw = yacc[:, cc] + grow[:, cc] * yrecv[q, :, 128 * c:128 * (c + 1)].astype(F32)
            ssm[:, cc] = (raw * (g / (1.0 + jnp.exp(-g)))).astype(BF16)
    p_copies = []
    for k in range(ncol):
        cc = slice(k * cols, (k + 1) * cols)
        value = part[:, cc] + dot(ssm[...], ws[:, cc])
        part[:, cc] = value
        psend[k] = value.astype(BF16)
        for d, p in enumerate(tp_peers):
            c = copy(
                psend.at[k, own_rows(p)], precv.at[d, :, k * cols:(k + 1) * cols],
                p_s.at[d, k], p_r.at[d, k], (s, p),
            )
            c.start()
            p_copies.append((d, k, c))
    keep = pltpu.make_async_copy(part.at[own_rows(t)], out_ref, o_s)
    keep.start()
    for _, _, c in p_copies:
        c.wait_recv()
    keep.wait()

    for c in swaps + b_moves + c_moves + x_copies + y_copies + [c for _, _, c in p_copies]:
        c.wait_send()

    @pl.loop(z + 1, planes)
    def _(zz):
        up(zz).wait_send()

    @pl.loop(0, z + 1)
    def _(zz):
        for c in kv_moves(zz):
            c.wait_send()

    @pl.when(z < planes - 1)
    def _():
        for c in range(nch):
            chain(c).wait_send()


def local(
    n, tp,
    queries, key_rows, value_rows, ssm_input, gate_input, write_vectors, read_vectors,
    decay_rates, attn_out_weight, ssm_out_weight,
):
    rows = queries.shape[0]
    width = ssm_input.shape[1]
    heads = decay_rates.shape[1]
    state = write_vectors.shape[1]
    model = attn_out_weight.shape[1]
    nq = queries.shape[1] // HEAD // tp
    planes = n // PLANE
    own = rows // tp
    span, _ = quarter_starts(width)
    nch = span // 128
    ncol = 4
    cols = model // ncol
    peers = PLANE - 1
    vmem = pltpu.VMEM
    dma = pltpu.SemaphoreType.DMA
    mine, others = pl.pallas_call(
        functools.partial(kernel, n, tp, heads, nq),
        out_shape=(
            jax.ShapeDtypeStruct((own, model), F32),
            jax.ShapeDtypeStruct((tp - 1, own, model), BF16),
        ),
        in_specs=[pl.BlockSpec(memory_space=pltpu.VMEM)] * 8
        + [pl.BlockSpec(memory_space=pl.ANY)] * 2,
        out_specs=(pl.BlockSpec(memory_space=pl.ANY),) * 2,
        scratch_shapes=[
            vmem(attn_out_weight.shape, BF16),
            vmem(ssm_out_weight.shape, BF16),
            vmem((n, 2, rows, HEAD), BF16),
            vmem((PLANE, 2, rows, state), BF16),
            vmem((PLANE, rows, span), BF16),
            vmem((PLANE, rows, span), BF16),
            vmem((PLANE, 8, span), F32),
            vmem((PLANE + 1, 8, span), F32),
            vmem((PLANE, state, span), F32),
            vmem((1, state, span), F32),
            vmem((nch, state, 128), BF16),
            vmem((nch, state, 128), BF16),
            vmem((PLANE, rows, span), BF16),
            vmem((PLANE, rows, span), BF16),
            vmem((ncol, rows, cols), BF16),
            vmem((nq * rows, HEAD), BF16),
            vmem((rows, nq * HEAD), BF16),
            vmem((rows, width), F32),
            vmem((rows, width), F32),
            vmem((rows, model), F32),
            vmem((rows, width), BF16),
            vmem((nq * rows, HEAD), F32),
            vmem((nq * rows, HEAD), F32),
            vmem((nq * rows, HEAD), F32),
            dma((2,)),
            dma((2, tp - 1)),
            dma((2, tp - 1)),
            dma((planes,)),
            dma((planes,)),
            dma((planes, peers)),
            dma((planes, peers)),
            dma((2, peers)),
            dma((2, peers)),
            dma((peers,)),
            dma((peers,)),
            dma((peers,)),
            dma((peers,)),
            dma((nch,)),
            dma((nch,)),
            dma((peers,)),
            dma((peers,)),
            dma((tp - 1, ncol)),
            dma((tp - 1, ncol)),
            dma,
        ],
        compiler_params=pltpu.CompilerParams(
            collective_id=0, has_side_effects=True, vmem_limit_bytes=56 * 1024 * 1024
        ),
    )(
        queries, key_rows, value_rows, ssm_input, gate_input, write_vectors, read_vectors,
        decay_rates.T, attn_out_weight, ssm_out_weight,
    )
    for d in range(tp - 1):
        mine = mine + others[d].astype(F32)
    return mine


def solution(mesh):
    placed = (
        P("seq", None),
        P(("seq", "tp"), None),
        P(("seq", "tp"), None),
        P("seq", "tp"),
        P("seq", "tp"),
        P("seq", None),
        P("seq", None),
        P("seq", "tp"),
        P("tp", None),
        P("tp", None),
    )
    body = functools.partial(local, mesh.shape["seq"], mesh.shape["tp"])
    return jax.shard_map(
        body, mesh=mesh, in_specs=placed, out_specs=P(("seq", "tp"), None), check_vma=False
    )
```

```python
import functools
import math

import jax
import jax.numpy as jnp
from jax import lax
from jax.experimental import pallas as pl
from jax.experimental.pallas import tpu as pltpu
from jax.sharding import PartitionSpec as P

KVHEADS = 2
HEAD = 128
HDIM = 64
PLANE = 4
MESH = pl.DeviceIdType.MESH
F32 = jnp.float32
BF16 = jnp.bfloat16
PRECISE = lax.Precision.HIGHEST


def dot(a, b):
    return jnp.dot(a, b, preferred_element_type=F32)


def dot_tn(a, b, precision=None):
    dims = (((0,), (0,)), ((), ()))
    return lax.dot_general(a, b, dims, precision=precision, preferred_element_type=F32)


def dot_nt(a, b, precision=None):
    dims = (((1,), (1,)), ((), ()))
    return lax.dot_general(a, b, dims, precision=precision, preferred_element_type=F32)


def quarter_starts(width):
    span = -(-width // (PLANE * 128)) * 128
    return span, [min(q * span, width - span) for q in range(PLANE)]


def kernel(
    n, tp, heads, nq,
    q_ref, k_ref, v_ref, x_ref, gate_ref, b_ref, c_ref, rate_ref, wa_hbm, ws_hbm,
    out_ref, precv,
    wa, ws, kv, bc, xr, rr, grown, dr, loc, tot, er, es, ysend, yrecv, psend,
    qs, attn, yacc, grow, part, ssm, acc, peak, norm,
    wsem, swap_s, swap_r, col_s, col_r, pl_s, pl_r, bc_s, bc_r, x_s, x_r, d_s, d_r,
    e_s, e_r, y_s, y_r, p_s, p_r, o_s,
):
    s = lax.axis_index("seq")
    t = lax.axis_index("tp")
    planes = n // PLANE
    z = s // PLANE
    i = s % PLANE
    rows = q_ref.shape[0]
    width = x_ref.shape[1]
    model = wa.shape[1]
    own = rows // tp
    span, starts = quarter_starts(width)
    nch = span // 128
    ncol = psend.shape[0]
    cols = model // ncol

    def copy(src, dst, send, recv, to):
        return pltpu.make_async_remote_copy(
            src_ref=src, dst_ref=dst, send_sem=send, recv_sem=recv,
            device_id=to, device_id_type=MESH,
        )

    tiles = []
    for c in range(nch):
        seen = [lo for step in tiles for _, lo in step]
        step = []
        for q in range(PLANE):
            lo = starts[q] + 128 * c
            if lo not in seen:
                step.append((q, lo))
                seen.append(lo)
        tiles.append(step)
    order = [lo for step in tiles for _, lo in step]
    w_copies = [pltpu.make_async_copy(wa_hbm, wa, wsem.at[len(order)])] + [
        pltpu.make_async_copy(
            ws_hbm.at[pl.ds(lo, 128)], ws.at[pl.ds(128 * k, 128)], wsem.at[k]
        )
        for k, lo in enumerate(order)
    ]
    for w in w_copies:
        w.start()

    sib = i + 1 - 2 * (i % 2)
    ynb = (i + 2) % PLANE
    dia = (sib + 2) % PLANE
    plane_index = [ynb, dia, sib]
    plane_peers = [z * PLANE + j for j in plane_index]
    tp_peers = [(t + d) % tp for d in range(1, tp)]
    col_peers = [((z + d) % planes) * PLANE + i for d in range(1, planes)]

    barrier = pltpu.get_barrier_semaphore()
    for p in plane_peers + col_peers:
        pl.semaphore_signal(barrier, inc=1, device_id=(p, t), device_id_type=MESH)
    for p in tp_peers:
        pl.semaphore_signal(barrier, inc=1, device_id=(s, p), device_id_type=MESH)
    pl.semaphore_wait(barrier, len(plane_peers) + len(col_peers) + len(tp_peers))

    def relay(ref_of, send, recv):
        def move(block, kind, to):
            ref = ref_of(block)
            return copy(ref, ref, send.at[kind], recv.at[kind], (z * PLANE + to, t))
        return [move(i, 0, sib), move(i, 1, ynb), move(ynb, 2, sib)]

    bc[i, 0] = b_ref[...]
    bc[i, 1] = c_ref[...]
    b_moves = relay(lambda j: bc.at[j, 0], bc_s.at[0], bc_r.at[0])
    c_moves = relay(lambda j: bc.at[j, 1], bc_s.at[1], bc_r.at[1])
    b_moves[1].start()
    b_moves[0].start()

    def quarter(q):
        return pl.ds(pl.multiple_of(jnp.minimum(q * span, width - span), 128), span)

    r_copies = [
        copy(rate_ref, rr.at[i], d_s.at[d], d_r.at[d], (p, t))
        for d, p in enumerate(plane_peers)
    ]
    x_copies = [
        copy(x_ref.at[:, quarter(plane_index[d])], xr.at[i], x_s.at[d], x_r.at[d], (p, t))
        for d, p in enumerate(plane_peers)
    ]
    for c in r_copies + x_copies:
        c.start()
    c_moves[1].start()
    c_moves[0].start()
    xr[i] = x_ref[:, quarter(i)]
    rr[i] = rate_ref[...]

    def kv_cols(peer):
        return pl.ds(pl.multiple_of(peer * KVHEADS // tp * HEAD, HEAD), HEAD)

    def own_rows(peer):
        return pl.ds(pl.multiple_of(peer * own, own), own)

    swaps = []
    for d, p in enumerate(tp_peers):
        for m, ref in enumerate((k_ref, v_ref)):
            swaps.append(copy(
                ref.at[:, kv_cols(p)], kv.at[s, m, own_rows(t)],
                swap_s.at[m, d], swap_r.at[m, d], (s, p),
            ))
    for c in swaps:
        c.start()
    for m, ref in enumerate((k_ref, v_ref)):
        kv[s, m, own_rows(t), :] = ref[:, kv_cols(t)]

    row_id = lax.broadcasted_iota(jnp.int32, (rows, rows), 0)
    col_id = lax.broadcasted_iota(jnp.int32, (rows, rows), 1)
    causal = row_id >= col_id
    lower = jnp.where(causal, 1.0, 0.0).astype(F32)
    upper = jnp.where(row_id <= col_id, 1.0, 0.0).astype(F32)
    rates = -rate_ref[...]
    cum_t = jnp.dot(rates, upper, precision=PRECISE, preferred_element_type=F32)
    cum = dot_nt(lower, rates, PRECISE)
    from_start = jnp.exp(cum)
    first_half = lax.broadcasted_iota(jnp.int32, (rows, 128), 1) < HDIM

    def pair_cols(value, pair):
        a = value[:, 2 * pair:2 * pair + 1]
        b = value[:, 2 * pair + 1:2 * pair + 2]
        return jnp.where(first_half, a, b)

    for c in swaps:
        c.wait_recv()

    def kv_moves(zz):
        return relay(lambda j: kv.at[zz * PLANE + j], pl_s.at[zz], pl_r.at[zz])

    def up(zz):
        src = kv.at[s]
        return copy(src, src, col_s.at[zz], col_r.at[z], (zz * PLANE + i, t))

    def col_from(zz):
        src = kv.at[zz * PLANE + i]
        return copy(src, src, col_s.at[zz], col_r.at[zz], (s, t))

    @pl.loop(z + 1, planes)
    def _(zz):
        up(zz).start()

    for c in kv_moves(z)[:2]:
        c.start()

    b_moves[1].wait_recv()
    b_moves[2].start()

    read_write = dot_nt(c_ref[...], b_ref[...])
    for pair in range(width // 128):
        cc = slice(128 * pair, 128 * (pair + 1))
        factors = []
        for h in (2 * pair, 2 * pair + 1):
            gap = jnp.minimum(cum[:, h:h + 1] - cum_t[h:h + 1, :], 0.0)
            factors.append(jnp.where(causal, jnp.exp(gap) * read_write, 0.0).astype(BF16))
        x = x_ref[:, cc]
        zero = jnp.zeros_like(x)
        stacked = jnp.concatenate(
            [jnp.where(first_half, x, zero), jnp.where(first_half, zero, x)], axis=0
        )
        yacc[:, cc] = dot(jnp.concatenate(factors, axis=1), stacked)
        grow[:, cc] = pair_cols(from_start, pair)

    for c in r_copies:
        c.wait_recv()
    channel = lax.broadcasted_iota(jnp.int32, (heads, span), 1)
    head = (channel + jnp.minimum(i * span, width - span)) // HDIM
    pick = (lax.broadcasted_iota(jnp.int32, (heads, span), 0) == head).astype(F32)
    for j in range(PLANE):
        sums = dot_nt(lower, -rr[j], PRECISE)
        end = sums[rows - 1:rows, :]
        to_end = jnp.exp(end - sums)
        grown[j] = jnp.dot(to_end, pick, precision=PRECISE, preferred_element_type=F32)
        ends = jnp.broadcast_to(jnp.exp(end), (8, heads))
        dr[j] = jnp.dot(ends, pick, precision=PRECISE, preferred_element_type=F32)
    c_moves[1].wait_recv()
    c_moves[2].start()
    for c in [b_moves[0], b_moves[2]] + x_copies:
        c.wait_recv()
    total = jnp.zeros((bc.shape[3], span), F32)
    decay = jnp.ones((1, span), F32)
    for j in range(PLANE):
        scaled = (xr[j].astype(F32) * grown[j]).astype(BF16)
        block = dot_tn(bc[j, 0], scaled)
        loc[j] = block
        total = dr[j, 0:1, :] * total + block
        decay = decay * dr[j, 0:1, :]
    tot[0] = total
    dr[PLANE] = jnp.broadcast_to(decay, (8, span))

    def chain(c):
        to = (jnp.minimum(z + 1, planes - 1) * PLANE + i, t)
        return copy(es.at[c], er.at[c], e_s.at[c], e_r.at[c], to)

    @pl.when(z == 0)
    def _():
        er[...] = jnp.zeros_like(er)

    @pl.loop(0, z)
    def _(zz):
        col_from(zz).wait_recv()
        for c in kv_moves(zz)[:2]:
            c.start()

    @pl.when(z == 0)
    def _():
        for c in range(nch):
            es[c] = tot[0, :, 128 * c:128 * (c + 1)].astype(BF16)
            chain(c).start()

    @pl.loop(0, z + 1)
    def _(zz):
        moves = kv_moves(zz)
        moves[1].wait_recv()
        moves[2].start()

    for h in range(nq):
        lo = pl.multiple_of((t * nq + h) * HEAD, HEAD)
        qs[h * rows:(h + 1) * rows, :] = q_ref[:, pl.ds(lo, HEAD)]
    stack = nq * rows
    acc[...] = jnp.zeros_like(acc)
    norm[...] = jnp.zeros_like(norm)
    peak[...] = jnp.full_like(peak, -1e30)
    scale = 1.0 / math.sqrt(HEAD)
    wide = PLANE * rows

    def attend(zz, masked):
        moves = kv_moves(zz)
        moves[0].wait_recv()
        moves[2].wait_recv()
        keys = kv[pl.ds(zz * PLANE, PLANE), 0].reshape(wide, HEAD)
        vals = kv[pl.ds(zz * PLANE, PLANE), 1].reshape(wide, HEAD)
        for h in range(nq):
            hh = slice(h * rows, (h + 1) * rows)
            scores = dot_nt(qs[hh, :], keys) * scale
            if masked:
                key_id = lax.broadcasted_iota(jnp.int32, (rows, wide), 1)
                query_id = lax.broadcasted_iota(jnp.int32, (rows, wide), 0) + i * rows
                scores = jnp.where(key_id <= query_id, scores, -1e30)
            old = peak[hh, 0:1]
            new = jnp.maximum(old, jnp.max(scores, axis=1, keepdims=True))
            weights = jnp.exp(scores - new)
            shrink = jnp.exp(old - new)
            norm[hh, 0:1] = norm[hh, 0:1] * shrink + jnp.sum(weights, axis=1, keepdims=True)
            acc[hh, :] = acc[hh, :] * shrink + dot(weights.astype(BF16), vals)
            peak[hh, 0:1] = new

    early = z // 2 + (z // (planes - 1)) * (z - z // 2)

    @pl.loop(0, early)
    def _(zz):
        attend(zz, False)

    c_moves[0].wait_recv()
    c_moves[2].wait_recv()
    y_copies = []
    for c in range(nch):
        cc = slice(128 * c, 128 * (c + 1))

        @pl.when(z > 0)
        def _():
            chain(c).wait_recv()

        @pl.when((z > 0) & (z < planes - 1))
        def _():
            entering = er[c].astype(F32)
            es[c] = (dr[PLANE, 0:1, cc] * entering + tot[0, :, cc]).astype(BF16)
            chain(c).start()

        state = er[c].astype(F32)
        for j in range(PLANE):
            ysend[c, j] = dot(bc[j, 1], state.astype(BF16)).astype(BF16)
            if j < PLANE - 1:
                state = dr[j, 0:1, cc] * state + loc[j, :, cc]
        sends = [
            copy(ysend.at[c, plane_index[d]], yrecv.at[c, i], y_s.at[c, d], y_r.at[c, d], (p, t))
            for d, p in enumerate(plane_peers)
        ]
        for m in sends:
            m.start()
        y_copies.append(sends)
        yrecv[c, i] = ysend[c, i]

    attend(z, True)

    @pl.loop(early, z)
    def _(zz):
        attend(zz, False)

    for h in range(nq):
        hh = slice(h * rows, (h + 1) * rows)
        attn[:, h * HEAD:(h + 1) * HEAD] = (acc[hh, :] / norm[hh, 0:1]).astype(BF16)
    for w in w_copies:
        w.wait()
    for k in range(ncol):
        cc = slice(k * cols, (k + 1) * cols)
        part[:, cc] = dot(attn[...], wa[:, cc])

    p_copies = []
    done = 0
    for step in range(nch):
        for m in y_copies[step]:
            m.wait_recv()
        depth = 128 * len(tiles[step])
        for k, (q, lo) in enumerate(tiles[step]):
            cc = slice(lo, lo + 128)
            g = gate_ref[:, cc].astype(F32)
            raw = yacc[:, cc] + grow[:, cc] * yrecv[step, q].astype(F32)
            at = done + 128 * k
            ssm[:, at:at + 128] = (raw * (g / (1.0 + jnp.exp(-g)))).astype(BF16)
        for k in range(ncol):
            cc = slice(k * cols, (k + 1) * cols)
            value = part[:, cc] + dot(ssm[:, done:done + depth], ws[done:done + depth, cc])
            part[:, cc] = value
            if step == nch - 1:
                psend[k] = value.astype(BF16)
                for d, p in enumerate(tp_peers):
                    c = copy(
                        psend.at[k, own_rows(p)], precv.at[d, :, k * cols:(k + 1) * cols],
                        p_s.at[d, k], p_r.at[d, k], (s, p),
                    )
                    c.start()
                    p_copies.append((d, k, c))
        done += depth
    keep = pltpu.make_async_copy(part.at[own_rows(t)], out_ref, o_s)
    keep.start()
    for _, _, c in p_copies:
        c.wait_recv()
    keep.wait()

    moved = swaps + b_moves + c_moves + r_copies + x_copies + sum(y_copies, [])
    for c in moved + [c for _, _, c in p_copies]:
        c.wait_send()

    @pl.loop(z + 1, planes)
    def _(zz):
        up(zz).wait_send()

    @pl.loop(0, z + 1)
    def _(zz):
        for c in kv_moves(zz):
            c.wait_send()

    @pl.when(z < planes - 1)
    def _():
        for c in range(nch):
            chain(c).wait_send()


def local(
    n, tp,
    queries, key_rows, value_rows, ssm_input, gate_input, write_vectors, read_vectors,
    decay_rates, attn_out_weight, ssm_out_weight,
):
    rows = queries.shape[0]
    width = ssm_input.shape[1]
    heads = decay_rates.shape[1]
    state = write_vectors.shape[1]
    model = attn_out_weight.shape[1]
    nq = queries.shape[1] // HEAD // tp
    planes = n // PLANE
    own = rows // tp
    span, _ = quarter_starts(width)
    nch = span // 128
    ncol = 4
    cols = model // ncol
    peers = PLANE - 1
    vmem = pltpu.VMEM
    dma = pltpu.SemaphoreType.DMA
    mine, others = pl.pallas_call(
        functools.partial(kernel, n, tp, heads, nq),
        out_shape=(
            jax.ShapeDtypeStruct((own, model), F32),
            jax.ShapeDtypeStruct((tp - 1, own, model), BF16),
        ),
        in_specs=[pl.BlockSpec(memory_space=pltpu.VMEM)] * 8
        + [pl.BlockSpec(memory_space=pl.ANY)] * 2,
        out_specs=(pl.BlockSpec(memory_space=pl.ANY),) * 2,
        scratch_shapes=[
            vmem(attn_out_weight.shape, BF16),
            vmem(ssm_out_weight.shape, BF16),
            vmem((n, 2, rows, HEAD), BF16),
            vmem((PLANE, 2, rows, state), BF16),
            vmem((PLANE, rows, span), BF16),
            vmem((PLANE, heads, rows), F32),
            vmem((PLANE, rows, span), F32),
            vmem((PLANE + 1, 8, span), F32),
            vmem((PLANE, state, span), F32),
            vmem((1, state, span), F32),
            vmem((nch, state, 128), BF16),
            vmem((nch, state, 128), BF16),
            vmem((nch, PLANE, rows, 128), BF16),
            vmem((nch, PLANE, rows, 128), BF16),
            vmem((ncol, rows, cols), BF16),
            vmem((nq * rows, HEAD), BF16),
            vmem((rows, nq * HEAD), BF16),
            vmem((rows, width), F32),
            vmem((rows, width), F32),
            vmem((rows, model), F32),
            vmem((rows, width), BF16),
            vmem((nq * rows, HEAD), F32),
            vmem((nq * rows, HEAD), F32),
            vmem((nq * rows, HEAD), F32),
            dma((width // 128 + 1,)),
            dma((2, tp - 1)),
            dma((2, tp - 1)),
            dma((planes,)),
            dma((planes,)),
            dma((planes, peers)),
            dma((planes, peers)),
            dma((2, peers)),
            dma((2, peers)),
            dma((peers,)),
            dma((peers,)),
            dma((peers,)),
            dma((peers,)),
            dma((nch,)),
            dma((nch,)),
            dma((nch, peers)),
            dma((nch, peers)),
            dma((tp - 1, ncol)),
            dma((tp - 1, ncol)),
            dma,
        ],
        compiler_params=pltpu.CompilerParams(
            collective_id=0, has_side_effects=True, vmem_limit_bytes=56 * 1024 * 1024
        ),
    )(
        queries, key_rows, value_rows, ssm_input, gate_input, write_vectors, read_vectors,
        decay_rates.T, attn_out_weight, ssm_out_weight,
    )
    for d in range(tp - 1):
        mine = mine + others[d].astype(F32)
    return mine


def solution(mesh):
    placed = (
        P("seq", None),
        P(("seq", "tp"), None),
        P(("seq", "tp"), None),
        P("seq", "tp"),
        P("seq", "tp"),
        P("seq", None),
        P("seq", None),
        P("seq", "tp"),
        P("tp", None),
        P("tp", None),
    )
    body = functools.partial(local, mesh.shape["seq"], mesh.shape["tp"])
    return jax.shard_map(
        body, mesh=mesh, in_specs=placed, out_specs=P(("seq", "tp"), None), check_vma=False
    )
```

```python
import functools
import math

import jax
import jax.numpy as jnp
from jax import lax
from jax.experimental import pallas as pl
from jax.experimental.pallas import tpu as pltpu
from jax.sharding import PartitionSpec as P

KVHEADS = 2
HEAD = 128
HDIM = 64
PLANE = 4
MESH = pl.DeviceIdType.MESH
F32 = jnp.float32
BF16 = jnp.bfloat16
PRECISE = lax.Precision.HIGHEST


def dot(a, b):
    return jnp.dot(a, b, preferred_element_type=F32)


def dot_tn(a, b, precision=None):
    dims = (((0,), (0,)), ((), ()))
    return lax.dot_general(a, b, dims, precision=precision, preferred_element_type=F32)


def dot_nt(a, b, precision=None):
    dims = (((1,), (1,)), ((), ()))
    return lax.dot_general(a, b, dims, precision=precision, preferred_element_type=F32)


def quarter_starts(width):
    span = -(-width // (PLANE * 128)) * 128
    return span, [min(q * span, width - span) for q in range(PLANE)]


def kernel(
    n, tp, heads, nq,
    q_ref, k_ref, v_ref, x_ref, gate_ref, b_ref, c_ref, rate_ref, wa_hbm, ws_hbm,
    out_ref, precv,
    wa, ws, kv, bc, xr, rr, dr, loc, tot, er, es, ysend, yrecv, psend,
    qs, attn, yacc, grow, part, ssm, acc, peak, norm,
    wsem, swap_s, swap_r, col_s, col_r, pl_s, pl_r, bc_s, bc_r, x_s, x_r, d_s, d_r,
    e_s, e_r, y_s, y_r, p_s, p_r, o_s,
):
    s = lax.axis_index("seq")
    t = lax.axis_index("tp")
    planes = n // PLANE
    z = s // PLANE
    i = s % PLANE
    rows = q_ref.shape[0]
    width = x_ref.shape[1]
    model = wa.shape[1]
    own = rows // tp
    span, starts = quarter_starts(width)
    nch = span // 128
    ncol = psend.shape[0]
    cols = model // ncol

    def copy(src, dst, send, recv, to):
        return pltpu.make_async_remote_copy(
            src_ref=src, dst_ref=dst, send_sem=send, recv_sem=recv,
            device_id=to, device_id_type=MESH,
        )

    tiles = []
    for c in range(nch):
        seen = [lo for step in tiles for _, lo in step]
        step = []
        for q in range(PLANE):
            lo = starts[q] + 128 * c
            if lo not in seen:
                step.append((q, lo))
                seen.append(lo)
        tiles.append(step)
    order = [lo for step in tiles for _, lo in step]
    w_copies = [pltpu.make_async_copy(wa_hbm, wa, wsem.at[len(order)])] + [
        pltpu.make_async_copy(
            ws_hbm.at[pl.ds(lo, 128)], ws.at[pl.ds(128 * k, 128)], wsem.at[k]
        )
        for k, lo in enumerate(order)
    ]
    for w in w_copies:
        w.start()

    sib = i + 1 - 2 * (i % 2)
    ynb = (i + 2) % PLANE
    dia = (sib + 2) % PLANE
    plane_index = [ynb, dia, sib]
    plane_peers = [z * PLANE + j for j in plane_index]
    tp_peers = [(t + d) % tp for d in range(1, tp)]
    col_peers = [((z + d) % planes) * PLANE + i for d in range(1, planes)]

    barrier = pltpu.get_barrier_semaphore()
    for p in plane_peers + col_peers:
        pl.semaphore_signal(barrier, inc=1, device_id=(p, t), device_id_type=MESH)
    for p in tp_peers:
        pl.semaphore_signal(barrier, inc=1, device_id=(s, p), device_id_type=MESH)
    pl.semaphore_wait(barrier, len(plane_peers) + len(col_peers) + len(tp_peers))

    def relay(ref_of, send, recv):
        def move(block, kind, to):
            ref = ref_of(block)
            return copy(ref, ref, send.at[kind], recv.at[kind], (z * PLANE + to, t))
        return [move(i, 0, sib), move(i, 1, ynb), move(ynb, 2, sib)]

    bc[i, 0] = b_ref[...]
    bc[i, 1] = c_ref[...]
    b_moves = relay(lambda j: bc.at[j, 0], bc_s.at[0], bc_r.at[0])
    c_moves = relay(lambda j: bc.at[j, 1], bc_s.at[1], bc_r.at[1])
    b_moves[1].start()
    b_moves[0].start()

    def quarter(q):
        return pl.ds(pl.multiple_of(jnp.minimum(q * span, width - span), 128), span)

    r_copies = [
        copy(rate_ref, rr.at[i], d_s.at[d], d_r.at[d], (p, t))
        for d, p in enumerate(plane_peers)
    ]
    x_copies = [
        copy(x_ref.at[:, quarter(plane_index[d])], xr.at[i], x_s.at[d], x_r.at[d], (p, t))
        for d, p in enumerate(plane_peers)
    ]
    for c in r_copies + x_copies:
        c.start()
    c_moves[1].start()
    c_moves[0].start()
    xr[i] = x_ref[:, quarter(i)]
    rr[i] = rate_ref[...]

    def kv_cols(peer):
        return pl.ds(pl.multiple_of(peer * KVHEADS // tp * HEAD, HEAD), HEAD)

    def own_rows(peer):
        return pl.ds(pl.multiple_of(peer * own, own), own)

    swaps = []
    for d, p in enumerate(tp_peers):
        for m, ref in enumerate((k_ref, v_ref)):
            swaps.append(copy(
                ref.at[:, kv_cols(p)], kv.at[s, m, own_rows(t)],
                swap_s.at[m, d], swap_r.at[m, d], (s, p),
            ))
    for c in swaps:
        c.start()
    for m, ref in enumerate((k_ref, v_ref)):
        kv[s, m, own_rows(t), :] = ref[:, kv_cols(t)]

    row_id = lax.broadcasted_iota(jnp.int32, (rows, rows), 0)
    col_id = lax.broadcasted_iota(jnp.int32, (rows, rows), 1)
    causal = row_id >= col_id
    lower = jnp.where(causal, 1.0, 0.0).astype(F32)
    upper = jnp.where(row_id <= col_id, 1.0, 0.0).astype(F32)
    rates = -rate_ref[...]
    cum_t = jnp.dot(rates, upper, precision=PRECISE, preferred_element_type=F32)
    cum = dot_nt(lower, rates, PRECISE)
    from_start = jnp.exp(cum)
    first_half = lax.broadcasted_iota(jnp.int32, (rows, 128), 1) < HDIM

    def pair_cols(value, pair):
        a = value[:, 2 * pair:2 * pair + 1]
        b = value[:, 2 * pair + 1:2 * pair + 2]
        return jnp.where(first_half, a, b)

    for c in swaps:
        c.wait_recv()

    def kv_moves(zz):
        return relay(lambda j: kv.at[zz * PLANE + j], pl_s.at[zz], pl_r.at[zz])

    def up(zz):
        src = kv.at[s]
        return copy(src, src, col_s.at[zz], col_r.at[z], (zz * PLANE + i, t))

    def col_from(zz):
        src = kv.at[zz * PLANE + i]
        return copy(src, src, col_s.at[zz], col_r.at[zz], (s, t))

    @pl.loop(z + 1, planes)
    def _(zz):
        up(zz).start()

    for c in kv_moves(z)[:2]:
        c.start()

    b_moves[1].wait_recv()
    b_moves[2].start()

    for c in r_copies:
        c.wait_recv()
    channel = lax.broadcasted_iota(jnp.int32, (PLANE * heads, span), 1)
    head = (channel + jnp.minimum(i * span, width - span)) // HDIM
    line = lax.broadcasted_iota(jnp.int32, (PLANE * heads, span), 0)
    pick = jnp.concatenate(
        [(line == head + j * heads).astype(F32) for j in range(PLANE)], axis=1
    )
    sums = dot_nt(lower, -jnp.concatenate([rr[j] for j in range(PLANE)], axis=0), PRECISE)
    end = sums[rows - 1:rows, :]
    ends = jnp.broadcast_to(jnp.exp(end), (8, PLANE * heads))
    to_end = jnp.concatenate([jnp.exp(end - sums), ends], axis=0)
    spread = jnp.dot(to_end, pick, precision=PRECISE, preferred_element_type=F32)
    for j in range(PLANE):
        dr[j] = spread[rows:, span * j:span * (j + 1)]
    c_moves[1].wait_recv()
    c_moves[2].start()
    for c in [b_moves[0], b_moves[2]] + x_copies:
        c.wait_recv()
    total = jnp.zeros((bc.shape[3], span), F32)
    decay = jnp.ones((1, span), F32)
    for j in range(PLANE):
        scaled = (xr[j].astype(F32) * spread[:rows, span * j:span * (j + 1)]).astype(BF16)
        block = dot_tn(bc[j, 0], scaled)
        loc[j] = block
        total = dr[j, 0:1, :] * total + block
        decay = decay * dr[j, 0:1, :]
    tot[0] = total
    dr[PLANE] = jnp.broadcast_to(decay, (8, span))

    half = bc.shape[3] // 2
    pieces = [(c, m) for c in range(nch) for m in range(2)]

    def chain(c, m):
        to = (jnp.minimum(z + 1, planes - 1) * PLANE + i, t)
        ms = slice(half * m, half * (m + 1))
        return copy(es.at[c, ms], er.at[c, ms], e_s.at[c, m], e_r.at[c, m], to)

    @pl.when(z == 0)
    def _():
        er[...] = jnp.zeros_like(er)

    @pl.when(z == 0)
    def _():
        for c, m in pieces:
            ms = slice(half * m, half * (m + 1))
            es[c, ms, :] = tot[0, ms, 128 * c:128 * (c + 1)].astype(BF16)
            chain(c, m).start()

    @pl.loop(0, z)
    def _(zz):
        col_from(zz).wait_recv()
        for c in kv_moves(zz)[:2]:
            c.start()

    read_write = dot_nt(c_ref[...], b_ref[...])
    for pair in range(width // 128):
        cc = slice(128 * pair, 128 * (pair + 1))
        factors = []
        for h in (2 * pair, 2 * pair + 1):
            gap = jnp.minimum(cum[:, h:h + 1] - cum_t[h:h + 1, :], 0.0)
            factors.append(jnp.where(causal, jnp.exp(gap) * read_write, 0.0).astype(BF16))
        x = x_ref[:, cc]
        zero = jnp.zeros_like(x)
        stacked = jnp.concatenate(
            [jnp.where(first_half, x, zero), jnp.where(first_half, zero, x)], axis=0
        )
        yacc[:, cc] = dot(jnp.concatenate(factors, axis=1), stacked)
        grow[:, cc] = pair_cols(from_start, pair)

    @pl.loop(0, z + 1)
    def _(zz):
        moves = kv_moves(zz)
        moves[1].wait_recv()
        moves[2].start()

    for h in range(nq):
        lo = pl.multiple_of((t * nq + h) * HEAD, HEAD)
        qs[h * rows:(h + 1) * rows, :] = q_ref[:, pl.ds(lo, HEAD)]
    stack = nq * rows
    acc[...] = jnp.zeros_like(acc)
    norm[...] = jnp.zeros_like(norm)
    peak[...] = jnp.full_like(peak, -1e30)
    scale = 1.0 / math.sqrt(HEAD)
    wide = PLANE * rows

    def attend(zz, masked):
        moves = kv_moves(zz)
        moves[0].wait_recv()
        moves[2].wait_recv()
        keys = kv[pl.ds(zz * PLANE, PLANE), 0].reshape(wide, HEAD)
        vals = kv[pl.ds(zz * PLANE, PLANE), 1].reshape(wide, HEAD)
        for h in range(nq):
            hh = slice(h * rows, (h + 1) * rows)
            scores = dot_nt(qs[hh, :], keys) * scale
            if masked:
                key_id = lax.broadcasted_iota(jnp.int32, (rows, wide), 1)
                query_id = lax.broadcasted_iota(jnp.int32, (rows, wide), 0) + i * rows
                scores = jnp.where(key_id <= query_id, scores, -1e30)
            old = peak[hh, 0:1]
            new = jnp.maximum(old, jnp.max(scores, axis=1, keepdims=True))
            weights = jnp.exp(scores - new)
            shrink = jnp.exp(old - new)
            norm[hh, 0:1] = norm[hh, 0:1] * shrink + jnp.sum(weights, axis=1, keepdims=True)
            acc[hh, :] = acc[hh, :] * shrink + dot(weights.astype(BF16), vals)
            peak[hh, 0:1] = new

    early = z // 2 + (z // (planes - 1)) * (z - z // 2)

    @pl.loop(0, early)
    def _(zz):
        attend(zz, False)

    c_moves[0].wait_recv()
    c_moves[2].wait_recv()
    y_copies = []

    @pl.when((z > 0) & (z < planes - 1))
    def _():
        for c, m in pieces:
            cc = slice(128 * c, 128 * (c + 1))
            ms = slice(half * m, half * (m + 1))
            chain(c, m).wait_recv()
            entering = er[c, ms, :].astype(F32)
            es[c, ms, :] = (dr[PLANE, 0:1, cc] * entering + tot[0, ms, cc]).astype(BF16)
            chain(c, m).start()

    for c in range(nch):
        cc = slice(128 * c, 128 * (c + 1))

        @pl.when((z > 0) & (z == planes - 1))
        def _():
            for m in range(2):
                chain(c, m).wait_recv()

        state = er[c].astype(F32)
        for j in range(PLANE):
            ysend[c, j] = dot(bc[j, 1], state.astype(BF16)).astype(BF16)
            if j < PLANE - 1:
                state = dr[j, 0:1, cc] * state + loc[j, :, cc]
        sends = [
            copy(ysend.at[c, plane_index[d]], yrecv.at[c, i], y_s.at[c, d], y_r.at[c, d], (p, t))
            for d, p in enumerate(plane_peers)
        ]
        for m in sends:
            m.start()
        y_copies.append(sends)
        yrecv[c, i] = ysend[c, i]

    attend(z, True)

    @pl.loop(early, z)
    def _(zz):
        attend(zz, False)

    for h in range(nq):
        hh = slice(h * rows, (h + 1) * rows)
        attn[:, h * HEAD:(h + 1) * HEAD] = (acc[hh, :] / norm[hh, 0:1]).astype(BF16)
    for w in w_copies:
        w.wait()
    for k in range(ncol):
        cc = slice(k * cols, (k + 1) * cols)
        part[:, cc] = dot(attn[...], wa[:, cc])

    p_copies = []
    done = 0
    for step in range(nch):
        for m in y_copies[step]:
            m.wait_recv()
        depth = 128 * len(tiles[step])
        for k, (q, lo) in enumerate(tiles[step]):
            cc = slice(lo, lo + 128)
            g = gate_ref[:, cc].astype(F32)
            raw = yacc[:, cc] + grow[:, cc] * yrecv[step, q].astype(F32)
            at = done + 128 * k
            ssm[:, at:at + 128] = (raw * (g / (1.0 + jnp.exp(-g)))).astype(BF16)
        for k in range(ncol):
            cc = slice(k * cols, (k + 1) * cols)
            value = part[:, cc] + dot(ssm[:, done:done + depth], ws[done:done + depth, cc])
            part[:, cc] = value
            if step == nch - 1:
                psend[k] = value.astype(BF16)
                for d, p in enumerate(tp_peers):
                    c = copy(
                        psend.at[k, own_rows(p)], precv.at[d, :, k * cols:(k + 1) * cols],
                        p_s.at[d, k], p_r.at[d, k], (s, p),
                    )
                    c.start()
                    p_copies.append((d, k, c))
        done += depth
    keep = pltpu.make_async_copy(part.at[own_rows(t)], out_ref, o_s)
    keep.start()
    for _, _, c in p_copies:
        c.wait_recv()
    keep.wait()

    moved = swaps + b_moves + c_moves + r_copies + x_copies + sum(y_copies, [])
    for c in moved + [c for _, _, c in p_copies]:
        c.wait_send()

    @pl.loop(z + 1, planes)
    def _(zz):
        up(zz).wait_send()

    @pl.loop(0, z + 1)
    def _(zz):
        for c in kv_moves(zz):
            c.wait_send()

    @pl.when(z < planes - 1)
    def _():
        for c, m in pieces:
            chain(c, m).wait_send()


def local(
    n, tp,
    queries, key_rows, value_rows, ssm_input, gate_input, write_vectors, read_vectors,
    decay_rates, attn_out_weight, ssm_out_weight,
):
    rows = queries.shape[0]
    width = ssm_input.shape[1]
    heads = decay_rates.shape[1]
    state = write_vectors.shape[1]
    model = attn_out_weight.shape[1]
    nq = queries.shape[1] // HEAD // tp
    planes = n // PLANE
    own = rows // tp
    span, _ = quarter_starts(width)
    nch = span // 128
    ncol = 8
    cols = model // ncol
    peers = PLANE - 1
    vmem = pltpu.VMEM
    dma = pltpu.SemaphoreType.DMA
    mine, others = pl.pallas_call(
        functools.partial(kernel, n, tp, heads, nq),
        out_shape=(
            jax.ShapeDtypeStruct((own, model), F32),
            jax.ShapeDtypeStruct((tp - 1, own, model), BF16),
        ),
        in_specs=[pl.BlockSpec(memory_space=pltpu.VMEM)] * 8
        + [pl.BlockSpec(memory_space=pl.ANY)] * 2,
        out_specs=(pl.BlockSpec(memory_space=pl.ANY),) * 2,
        scratch_shapes=[
            vmem(attn_out_weight.shape, BF16),
            vmem(ssm_out_weight.shape, BF16),
            vmem((n, 2, rows, HEAD), BF16),
            vmem((PLANE, 2, rows, state), BF16),
            vmem((PLANE, rows, span), BF16),
            vmem((PLANE, heads, rows), F32),
            vmem((PLANE + 1, 8, span), F32),
            vmem((PLANE, state, span), F32),
            vmem((1, state, span), F32),
            vmem((nch, state, 128), BF16),
            vmem((nch, state, 128), BF16),
            vmem((nch, PLANE, rows, 128), BF16),
            vmem((nch, PLANE, rows, 128), BF16),
            vmem((ncol, rows, cols), BF16),
            vmem((nq * rows, HEAD), BF16),
            vmem((rows, nq * HEAD), BF16),
            vmem((rows, width), F32),
            vmem((rows, width), F32),
            vmem((rows, model), F32),
            vmem((rows, width), BF16),
            vmem((nq * rows, HEAD), F32),
            vmem((nq * rows, HEAD), F32),
            vmem((nq * rows, HEAD), F32),
            dma((width // 128 + 1,)),
            dma((2, tp - 1)),
            dma((2, tp - 1)),
            dma((planes,)),
            dma((planes,)),
            dma((planes, peers)),
            dma((planes, peers)),
            dma((2, peers)),
            dma((2, peers)),
            dma((peers,)),
            dma((peers,)),
            dma((peers,)),
            dma((peers,)),
            dma((nch, 2)),
            dma((nch, 2)),
            dma((nch, peers)),
            dma((nch, peers)),
            dma((tp - 1, ncol)),
            dma((tp - 1, ncol)),
            dma,
        ],
        compiler_params=pltpu.CompilerParams(
            collective_id=0, has_side_effects=True, vmem_limit_bytes=56 * 1024 * 1024
        ),
    )(
        queries, key_rows, value_rows, ssm_input, gate_input, write_vectors, read_vectors,
        decay_rates.T, attn_out_weight, ssm_out_weight,
    )
    for d in range(tp - 1):
        mine = mine + others[d].astype(F32)
    return mine


def solution(mesh):
    placed = (
        P("seq", None),
        P(("seq", "tp"), None),
        P(("seq", "tp"), None),
        P("seq", "tp"),
        P("seq", "tp"),
        P("seq", None),
        P("seq", None),
        P("seq", "tp"),
        P("tp", None),
        P("tp", None),
    )
    body = functools.partial(local, mesh.shape["seq"], mesh.shape["tp"])
    return jax.shard_map(
        body, mesh=mesh, in_specs=placed, out_specs=P(("seq", "tp"), None), check_vma=False
    )
```

```python
import functools
import math

import jax
import jax.numpy as jnp
from jax import lax
from jax.experimental import pallas as pl
from jax.experimental.pallas import tpu as pltpu
from jax.sharding import PartitionSpec as P

KVHEADS = 2
HEAD = 128
HDIM = 64
PLANE = 4
MESH = pl.DeviceIdType.MESH
F32 = jnp.float32
BF16 = jnp.bfloat16
PRECISE = lax.Precision.HIGHEST


def dot(a, b):
    return jnp.dot(a, b, preferred_element_type=F32)


def dot_tn(a, b, precision=None):
    dims = (((0,), (0,)), ((), ()))
    return lax.dot_general(a, b, dims, precision=precision, preferred_element_type=F32)


def dot_nt(a, b, precision=None):
    dims = (((1,), (1,)), ((), ()))
    return lax.dot_general(a, b, dims, precision=precision, preferred_element_type=F32)


def quarter_starts(width):
    span = -(-width // (PLANE * 128)) * 128
    return span, [min(q * span, width - span) for q in range(PLANE)]


def kernel(
    n, tp, heads, nq,
    q_in, k_in, v_in, x_in, gate_in, b_in, c_in, rate_in, wa_hbm, ws_hbm,
    out_ref, precv,
    q_ref, k_ref, v_ref, x_ref, gate_ref, b_ref, c_ref, rate_ref,
    wa, ws, kv, bc, xr, rr, dr, loc, tot, er, es, ysend, yrecv, psend,
    qs, attn, yacc, grow, part, ssm, acc, peak, norm,
    wsem, swap_s, swap_r, col_s, col_r, pl_s, pl_r, bc_s, bc_r, x_s, x_r, d_s, d_r,
    e_s, e_r, y_s, y_r, p_s, p_r, o_s, in_s,
):
    s = lax.axis_index("seq")
    t = lax.axis_index("tp")
    planes = n // PLANE
    z = s // PLANE
    i = s % PLANE
    rows = q_ref.shape[0]
    width = x_ref.shape[1]
    model = wa.shape[1]
    own = rows // tp
    span, starts = quarter_starts(width)
    nch = span // 128
    ncol = psend.shape[0]
    cols = model // ncol

    def copy(src, dst, send, recv, to):
        return pltpu.make_async_remote_copy(
            src_ref=src, dst_ref=dst, send_sem=send, recv_sem=recv,
            device_id=to, device_id_type=MESH,
        )

    tiles = []
    for c in range(nch):
        seen = [lo for step in tiles for _, lo in step]
        step = []
        for q in range(PLANE):
            lo = starts[q] + 128 * c
            if lo not in seen:
                step.append((q, lo))
                seen.append(lo)
        tiles.append(step)
    order = [lo for step in tiles for _, lo in step]
    w_copies = [pltpu.make_async_copy(wa_hbm, wa, wsem.at[len(order)])] + [
        pltpu.make_async_copy(
            ws_hbm.at[pl.ds(lo, 128)], ws.at[pl.ds(128 * k, 128)], wsem.at[k]
        )
        for k, lo in enumerate(order)
    ]
    fetch = [
        pltpu.make_async_copy(src, dst, in_s.at[k])
        for k, (src, dst) in enumerate((
            (b_in, b_ref), (rate_in, rate_ref), (x_in, x_ref), (c_in, c_ref),
            (k_in, k_ref), (v_in, v_ref), (q_in, q_ref), (gate_in, gate_ref),
        ))
    ]
    for c in fetch:
        c.start()

    sib = i + 1 - 2 * (i % 2)
    ynb = (i + 2) % PLANE
    dia = (sib + 2) % PLANE
    plane_index = [ynb, dia, sib]
    plane_peers = [z * PLANE + j for j in plane_index]
    tp_peers = [(t + d) % tp for d in range(1, tp)]
    col_peers = [((z + d) % planes) * PLANE + i for d in range(1, planes)]

    barrier = pltpu.get_barrier_semaphore()
    for p in plane_peers + col_peers:
        pl.semaphore_signal(barrier, inc=1, device_id=(p, t), device_id_type=MESH)
    for p in tp_peers:
        pl.semaphore_signal(barrier, inc=1, device_id=(s, p), device_id_type=MESH)
    for c in fetch:
        c.wait()
    pl.semaphore_wait(barrier, len(plane_peers) + len(col_peers) + len(tp_peers))

    def relay(ref_of, send, recv):
        def move(block, kind, to):
            ref = ref_of(block)
            return copy(ref, ref, send.at[kind], recv.at[kind], (z * PLANE + to, t))
        return [move(i, 0, sib), move(i, 1, ynb), move(ynb, 2, sib)]

    bc[i, 0] = b_ref[...]
    bc[i, 1] = c_ref[...]
    b_moves = relay(lambda j: bc.at[j, 0], bc_s.at[0], bc_r.at[0])
    c_moves = relay(lambda j: bc.at[j, 1], bc_s.at[1], bc_r.at[1])
    b_moves[1].start()
    b_moves[0].start()

    def quarter(q):
        return pl.ds(pl.multiple_of(jnp.minimum(q * span, width - span), 128), span)

    r_copies = [
        copy(rate_ref, rr.at[i], d_s.at[d], d_r.at[d], (p, t))
        for d, p in enumerate(plane_peers)
    ]
    x_copies = [
        copy(x_ref.at[:, quarter(plane_index[d])], xr.at[i], x_s.at[d], x_r.at[d], (p, t))
        for d, p in enumerate(plane_peers)
    ]
    for c in r_copies + x_copies:
        c.start()
    c_moves[1].start()
    c_moves[0].start()
    xr[i] = x_ref[:, quarter(i)]
    rr[i] = rate_ref[...]

    for w in w_copies:
        w.start()

    def kv_cols(peer):
        return pl.ds(pl.multiple_of(peer * KVHEADS // tp * HEAD, HEAD), HEAD)

    def own_rows(peer):
        return pl.ds(pl.multiple_of(peer * own, own), own)

    swaps = []
    for d, p in enumerate(tp_peers):
        for m, ref in enumerate((k_ref, v_ref)):
            swaps.append(copy(
                ref.at[:, kv_cols(p)], kv.at[s, m, own_rows(t)],
                swap_s.at[m, d], swap_r.at[m, d], (s, p),
            ))
    for c in swaps:
        c.start()
    for m, ref in enumerate((k_ref, v_ref)):
        kv[s, m, own_rows(t), :] = ref[:, kv_cols(t)]

    row_id = lax.broadcasted_iota(jnp.int32, (rows, rows), 0)
    col_id = lax.broadcasted_iota(jnp.int32, (rows, rows), 1)
    causal = row_id >= col_id
    lower = jnp.where(causal, 1.0, 0.0).astype(F32)
    upper = jnp.where(row_id <= col_id, 1.0, 0.0).astype(F32)
    rates = -rate_ref[...]
    cum_t = jnp.dot(rates, upper, precision=PRECISE, preferred_element_type=F32)
    cum = dot_nt(lower, rates, PRECISE)
    from_start = jnp.exp(cum)
    first_half = lax.broadcasted_iota(jnp.int32, (rows, 128), 1) < HDIM

    def pair_cols(value, pair):
        a = value[:, 2 * pair:2 * pair + 1]
        b = value[:, 2 * pair + 1:2 * pair + 2]
        return jnp.where(first_half, a, b)

    for c in swaps:
        c.wait_recv()

    def kv_moves(zz):
        return relay(lambda j: kv.at[zz * PLANE + j], pl_s.at[zz], pl_r.at[zz])

    def up(zz):
        src = kv.at[s]
        return copy(src, src, col_s.at[zz], col_r.at[z], (zz * PLANE + i, t))

    def col_from(zz):
        src = kv.at[zz * PLANE + i]
        return copy(src, src, col_s.at[zz], col_r.at[zz], (s, t))

    @pl.loop(z + 1, planes)
    def _(zz):
        up(zz).start()

    for c in kv_moves(z)[:2]:
        c.start()

    b_moves[1].wait_recv()
    b_moves[2].start()

    for c in r_copies:
        c.wait_recv()
    channel = lax.broadcasted_iota(jnp.int32, (PLANE * heads, span), 1)
    head = (channel + jnp.minimum(i * span, width - span)) // HDIM
    line = lax.broadcasted_iota(jnp.int32, (PLANE * heads, span), 0)
    pick = jnp.concatenate(
        [(line == head + j * heads).astype(F32) for j in range(PLANE)], axis=1
    )
    sums = dot_nt(lower, -jnp.concatenate([rr[j] for j in range(PLANE)], axis=0), PRECISE)
    end = sums[rows - 1:rows, :]
    ends = jnp.broadcast_to(jnp.exp(end), (8, PLANE * heads))
    to_end = jnp.concatenate([jnp.exp(end - sums), ends], axis=0)
    spread = jnp.dot(to_end, pick, precision=PRECISE, preferred_element_type=F32)
    for j in range(PLANE):
        dr[j] = spread[rows:, span * j:span * (j + 1)]
    c_moves[1].wait_recv()
    c_moves[2].start()
    for c in [b_moves[0], b_moves[2]] + x_copies:
        c.wait_recv()
    total = jnp.zeros((bc.shape[3], span), F32)
    decay = jnp.ones((1, span), F32)
    for j in range(PLANE):
        scaled = (xr[j].astype(F32) * spread[:rows, span * j:span * (j + 1)]).astype(BF16)
        block = dot_tn(bc[j, 0], scaled)
        loc[j] = block
        total = dr[j, 0:1, :] * total + block
        decay = decay * dr[j, 0:1, :]
    tot[0] = total
    dr[PLANE] = jnp.broadcast_to(decay, (8, span))

    half = bc.shape[3] // 2
    pieces = [(c, m) for c in range(nch) for m in range(2)]

    def chain(c, m):
        to = (jnp.minimum(z + 1, planes - 1) * PLANE + i, t)
        ms = slice(half * m, half * (m + 1))
        return copy(es.at[c, ms], er.at[c, ms], e_s.at[c, m], e_r.at[c, m], to)

    @pl.when(z == 0)
    def _():
        er[...] = jnp.zeros_like(er)

    @pl.when(z == 0)
    def _():
        for c, m in pieces:
            ms = slice(half * m, half * (m + 1))
            es[c, ms, :] = tot[0, ms, 128 * c:128 * (c + 1)].astype(BF16)
            chain(c, m).start()

    @pl.loop(0, z)
    def _(zz):
        col_from(zz).wait_recv()
        for c in kv_moves(zz)[:2]:
            c.start()

    read_write = dot_nt(c_ref[...], b_ref[...])
    for pair in range(width // 128):
        cc = slice(128 * pair, 128 * (pair + 1))
        factors = []
        for h in (2 * pair, 2 * pair + 1):
            gap = jnp.minimum(cum[:, h:h + 1] - cum_t[h:h + 1, :], 0.0)
            factors.append(jnp.where(causal, jnp.exp(gap) * read_write, 0.0).astype(BF16))
        x = x_ref[:, cc]
        zero = jnp.zeros_like(x)
        stacked = jnp.concatenate(
            [jnp.where(first_half, x, zero), jnp.where(first_half, zero, x)], axis=0
        )
        yacc[:, cc] = dot(jnp.concatenate(factors, axis=1), stacked)
        grow[:, cc] = pair_cols(from_start, pair)

    @pl.loop(0, z + 1)
    def _(zz):
        moves = kv_moves(zz)
        moves[1].wait_recv()
        moves[2].start()

    for h in range(nq):
        lo = pl.multiple_of((t * nq + h) * HEAD, HEAD)
        qs[h * rows:(h + 1) * rows, :] = q_ref[:, pl.ds(lo, HEAD)]
    stack = nq * rows
    acc[...] = jnp.zeros_like(acc)
    norm[...] = jnp.zeros_like(norm)
    peak[...] = jnp.full_like(peak, -1e30)
    scale = 1.0 / math.sqrt(HEAD)
    wide = PLANE * rows

    def attend(zz, masked):
        moves = kv_moves(zz)
        moves[0].wait_recv()
        moves[2].wait_recv()
        keys = kv[pl.ds(zz * PLANE, PLANE), 0].reshape(wide, HEAD)
        vals = kv[pl.ds(zz * PLANE, PLANE), 1].reshape(wide, HEAD)
        for h in range(nq):
            hh = slice(h * rows, (h + 1) * rows)
            scores = dot_nt(qs[hh, :], keys) * scale
            if masked:
                key_id = lax.broadcasted_iota(jnp.int32, (rows, wide), 1)
                query_id = lax.broadcasted_iota(jnp.int32, (rows, wide), 0) + i * rows
                scores = jnp.where(key_id <= query_id, scores, -1e30)
            old = peak[hh, 0:1]
            new = jnp.maximum(old, jnp.max(scores, axis=1, keepdims=True))
            weights = jnp.exp(scores - new)
            shrink = jnp.exp(old - new)
            norm[hh, 0:1] = norm[hh, 0:1] * shrink + jnp.sum(weights, axis=1, keepdims=True)
            acc[hh, :] = acc[hh, :] * shrink + dot(weights.astype(BF16), vals)
            peak[hh, 0:1] = new

    early = z // 2 + (z // (planes - 1)) * (z - z // 2)

    @pl.loop(0, early)
    def _(zz):
        attend(zz, False)

    c_moves[0].wait_recv()
    c_moves[2].wait_recv()
    y_copies = []

    @pl.when((z > 0) & (z < planes - 1))
    def _():
        for c, m in pieces:
            cc = slice(128 * c, 128 * (c + 1))
            ms = slice(half * m, half * (m + 1))
            chain(c, m).wait_recv()
            entering = er[c, ms, :].astype(F32)
            es[c, ms, :] = (dr[PLANE, 0:1, cc] * entering + tot[0, ms, cc]).astype(BF16)
            chain(c, m).start()

    for c in range(nch):
        cc = slice(128 * c, 128 * (c + 1))

        @pl.when((z > 0) & (z == planes - 1))
        def _():
            for m in range(2):
                chain(c, m).wait_recv()

        state = er[c].astype(F32)
        for j in range(PLANE):
            ysend[c, j] = dot(bc[j, 1], state.astype(BF16)).astype(BF16)
            if j < PLANE - 1:
                state = dr[j, 0:1, cc] * state + loc[j, :, cc]
        sends = [
            copy(ysend.at[c, plane_index[d]], yrecv.at[c, i], y_s.at[c, d], y_r.at[c, d], (p, t))
            for d, p in enumerate(plane_peers)
        ]
        for m in sends:
            m.start()
        y_copies.append(sends)
        yrecv[c, i] = ysend[c, i]

    attend(z, True)

    @pl.loop(early, z)
    def _(zz):
        attend(zz, False)

    for h in range(nq):
        hh = slice(h * rows, (h + 1) * rows)
        attn[:, h * HEAD:(h + 1) * HEAD] = (acc[hh, :] / norm[hh, 0:1]).astype(BF16)
    for w in w_copies:
        w.wait()
    for k in range(ncol):
        cc = slice(k * cols, (k + 1) * cols)
        part[:, cc] = dot(attn[...], wa[:, cc])

    p_copies = []
    done = 0
    for step in range(nch):
        for m in y_copies[step]:
            m.wait_recv()
        depth = 128 * len(tiles[step])
        for k, (q, lo) in enumerate(tiles[step]):
            cc = slice(lo, lo + 128)
            g = gate_ref[:, cc].astype(F32)
            raw = yacc[:, cc] + grow[:, cc] * yrecv[step, q].astype(F32)
            at = done + 128 * k
            ssm[:, at:at + 128] = (raw * (g / (1.0 + jnp.exp(-g)))).astype(BF16)
        for k in range(ncol):
            cc = slice(k * cols, (k + 1) * cols)
            value = part[:, cc] + dot(ssm[:, done:done + depth], ws[done:done + depth, cc])
            part[:, cc] = value
            if step == nch - 1:
                psend[k] = value.astype(BF16)
                for d, p in enumerate(tp_peers):
                    c = copy(
                        psend.at[k, own_rows(p)], precv.at[d, :, k * cols:(k + 1) * cols],
                        p_s.at[d, k], p_r.at[d, k], (s, p),
                    )
                    c.start()
                    p_copies.append((d, k, c))
        done += depth
    keep = pltpu.make_async_copy(part.at[own_rows(t)], out_ref, o_s)
    keep.start()
    for _, _, c in p_copies:
        c.wait_recv()
    keep.wait()

    moved = swaps + b_moves + c_moves + r_copies + x_copies + sum(y_copies, [])
    for c in moved + [c for _, _, c in p_copies]:
        c.wait_send()

    @pl.loop(z + 1, planes)
    def _(zz):
        up(zz).wait_send()

    @pl.loop(0, z + 1)
    def _(zz):
        for c in kv_moves(zz):
            c.wait_send()

    @pl.when(z < planes - 1)
    def _():
        for c, m in pieces:
            chain(c, m).wait_send()


def add_shares(mine_ref, others_ref, out_ref):
    total = mine_ref[...]
    for d in range(others_ref.shape[0]):
        total = total + others_ref[d].astype(F32)
    out_ref[...] = total


def local(
    n, tp,
    queries, key_rows, value_rows, ssm_input, gate_input, write_vectors, read_vectors,
    decay_rates, attn_out_weight, ssm_out_weight,
):
    rows = queries.shape[0]
    width = ssm_input.shape[1]
    heads = decay_rates.shape[1]
    state = write_vectors.shape[1]
    model = attn_out_weight.shape[1]
    nq = queries.shape[1] // HEAD // tp
    planes = n // PLANE
    own = rows // tp
    span, _ = quarter_starts(width)
    nch = span // 128
    ncol = 8
    cols = model // ncol
    peers = PLANE - 1
    vmem = pltpu.VMEM
    dma = pltpu.SemaphoreType.DMA
    mine, others = pl.pallas_call(
        functools.partial(kernel, n, tp, heads, nq),
        out_shape=(
            jax.ShapeDtypeStruct((own, model), F32),
            jax.ShapeDtypeStruct((tp - 1, own, model), BF16),
        ),
        in_specs=[pl.BlockSpec(memory_space=pl.ANY)] * 10,
        out_specs=(pl.BlockSpec(memory_space=pl.ANY),) * 2,
        scratch_shapes=[
            vmem(queries.shape, BF16),
            vmem(key_rows.shape, BF16),
            vmem(value_rows.shape, BF16),
            vmem(ssm_input.shape, BF16),
            vmem(gate_input.shape, BF16),
            vmem(write_vectors.shape, BF16),
            vmem(read_vectors.shape, BF16),
            vmem((heads, rows), F32),
            vmem(attn_out_weight.shape, BF16),
            vmem(ssm_out_weight.shape, BF16),
            vmem((n, 2, rows, HEAD), BF16),
            vmem((PLANE, 2, rows, state), BF16),
            vmem((PLANE, rows, span), BF16),
            vmem((PLANE, heads, rows), F32),
            vmem((PLANE + 1, 8, span), F32),
            vmem((PLANE, state, span), F32),
            vmem((1, state, span), F32),
            vmem((nch, state, 128), BF16),
            vmem((nch, state, 128), BF16),
            vmem((nch, PLANE, rows, 128), BF16),
            vmem((nch, PLANE, rows, 128), BF16),
            vmem((ncol, rows, cols), BF16),
            vmem((nq * rows, HEAD), BF16),
            vmem((rows, nq * HEAD), BF16),
            vmem((rows, width), F32),
            vmem((rows, width), F32),
            vmem((rows, model), F32),
            vmem((rows, width), BF16),
            vmem((nq * rows, HEAD), F32),
            vmem((nq * rows, HEAD), F32),
            vmem((nq * rows, HEAD), F32),
            dma((width // 128 + 1,)),
            dma((2, tp - 1)),
            dma((2, tp - 1)),
            dma((planes,)),
            dma((planes,)),
            dma((planes, peers)),
            dma((planes, peers)),
            dma((2, peers)),
            dma((2, peers)),
            dma((peers,)),
            dma((peers,)),
            dma((peers,)),
            dma((peers,)),
            dma((nch, 2)),
            dma((nch, 2)),
            dma((nch, peers)),
            dma((nch, peers)),
            dma((tp - 1, ncol)),
            dma((tp - 1, ncol)),
            dma,
            dma((8,)),
        ],
        compiler_params=pltpu.CompilerParams(
            collective_id=0, has_side_effects=True, vmem_limit_bytes=56 * 1024 * 1024
        ),
    )(
        queries, key_rows, value_rows, ssm_input, gate_input, write_vectors, read_vectors,
        decay_rates.T, attn_out_weight, ssm_out_weight,
    )
    return pl.pallas_call(
        add_shares,
        out_shape=jax.ShapeDtypeStruct((own, model), F32),
        in_specs=[pl.BlockSpec(memory_space=pltpu.VMEM)] * 2,
        out_specs=pl.BlockSpec(memory_space=pltpu.VMEM),
    )(mine, others)


def solution(mesh):
    placed = (
        P("seq", None),
        P(("seq", "tp"), None),
        P(("seq", "tp"), None),
        P("seq", "tp"),
        P("seq", "tp"),
        P("seq", None),
        P("seq", None),
        P("seq", "tp"),
        P("tp", None),
        P("tp", None),
    )
    body = functools.partial(local, mesh.shape["seq"], mesh.shape["tp"])
    return jax.shard_map(
        body, mesh=mesh, in_specs=placed, out_specs=P(("seq", "tp"), None), check_vma=False
    )
```

```python
import functools
import math

import jax
import jax.numpy as jnp
from jax import lax
from jax.experimental import pallas as pl
from jax.experimental.pallas import tpu as pltpu
from jax.sharding import PartitionSpec as P

KVHEADS = 2
HEAD = 128
HDIM = 64
PLANE = 4
MESH = pl.DeviceIdType.MESH
F32 = jnp.float32
BF16 = jnp.bfloat16
PRECISE = lax.Precision.HIGHEST


def dot(a, b):
    return jnp.dot(a, b, preferred_element_type=F32)


def dot_tn(a, b, precision=None):
    dims = (((0,), (0,)), ((), ()))
    return lax.dot_general(a, b, dims, precision=precision, preferred_element_type=F32)


def dot_nt(a, b, precision=None):
    dims = (((1,), (1,)), ((), ()))
    return lax.dot_general(a, b, dims, precision=precision, preferred_element_type=F32)


def quarter_starts(width):
    span = -(-width // (PLANE * 128)) * 128
    return span, [min(q * span, width - span) for q in range(PLANE)]


def kernel(
    n, tp, heads, nq,
    q_in, k_in, v_in, x_in, gate_in, b_in, c_in, rate_in, wa_hbm, ws_hbm,
    out_ref, precv,
    q_ref, k_ref, v_ref, x_ref, gate_ref, b_ref, c_ref, rate_ref,
    wa, ws, kv, bc, xr, rr, dr, loc, tot, er, es, ysend, yrecv, psend,
    qs, attn, yacc, grow, part, ssm, acc, peak, norm,
    wsem, swap_s, swap_r, col_s, col_r, pl_s, pl_r, bc_s, bc_r, x_s, x_r, d_s, d_r,
    e_s, e_r, y_s, y_r, p_s, p_r, o_s, in_s,
):
    s = lax.axis_index("seq")
    t = lax.axis_index("tp")
    planes = n // PLANE
    z = s // PLANE
    i = s % PLANE
    rows = q_ref.shape[0]
    width = x_ref.shape[1]
    model = wa.shape[1]
    own = rows // tp
    span, starts = quarter_starts(width)
    nch = span // 128
    ncol = psend.shape[0]
    cols = model // ncol

    def copy(src, dst, send, recv, to):
        return pltpu.make_async_remote_copy(
            src_ref=src, dst_ref=dst, send_sem=send, recv_sem=recv,
            device_id=to, device_id_type=MESH,
        )

    tiles = []
    for c in range(nch):
        seen = [lo for step in tiles for _, lo in step]
        step = []
        for q in range(PLANE):
            lo = starts[q] + 128 * c
            if lo not in seen:
                step.append((q, lo))
                seen.append(lo)
        tiles.append(step)
    order = [lo for step in tiles for _, lo in step]
    w_copies = [pltpu.make_async_copy(wa_hbm, wa, wsem.at[len(order)])] + [
        pltpu.make_async_copy(
            ws_hbm.at[pl.ds(lo, 128)], ws.at[pl.ds(128 * k, 128)], wsem.at[k]
        )
        for k, lo in enumerate(order)
    ]
    fetch = [
        pltpu.make_async_copy(src, dst, in_s.at[k])
        for k, (src, dst) in enumerate((
            (b_in, b_ref), (rate_in, rate_ref), (x_in, x_ref), (c_in, c_ref),
            (k_in, k_ref), (v_in, v_ref), (q_in, q_ref), (gate_in, gate_ref),
        ))
    ]
    for c in fetch:
        c.start()

    sib = i + 1 - 2 * (i % 2)
    ynb = (i + 2) % PLANE
    dia = (sib + 2) % PLANE
    plane_index = [ynb, dia, sib]
    plane_peers = [z * PLANE + j for j in plane_index]
    tp_peers = [(t + d) % tp for d in range(1, tp)]
    col_peers = [((z + d) % planes) * PLANE + i for d in range(1, planes)]

    barrier = pltpu.get_barrier_semaphore()
    for p in plane_peers + col_peers:
        pl.semaphore_signal(barrier, inc=1, device_id=(p, t), device_id_type=MESH)
    for p in tp_peers:
        pl.semaphore_signal(barrier, inc=1, device_id=(s, p), device_id_type=MESH)
    for c in fetch:
        c.wait()
    pl.semaphore_wait(barrier, len(plane_peers) + len(col_peers) + len(tp_peers))

    def relay(ref_of, send, recv):
        def move(block, kind, to):
            ref = ref_of(block)
            return copy(ref, ref, send.at[kind], recv.at[kind], (z * PLANE + to, t))
        return [move(i, 0, sib), move(i, 1, ynb), move(ynb, 2, sib)]

    bc[i, 0] = b_ref[...]
    bc[i, 1] = c_ref[...]
    b_moves = relay(lambda j: bc.at[j, 0], bc_s.at[0], bc_r.at[0])
    c_moves = relay(lambda j: bc.at[j, 1], bc_s.at[1], bc_r.at[1])
    b_moves[1].start()
    b_moves[0].start()

    def quarter(q):
        return pl.ds(pl.multiple_of(jnp.minimum(q * span, width - span), 128), span)

    r_copies = [
        copy(rate_ref, rr.at[i], d_s.at[d], d_r.at[d], (p, t))
        for d, p in enumerate(plane_peers)
    ]
    x_copies = [
        copy(x_ref.at[:, quarter(plane_index[d])], xr.at[i], x_s.at[d], x_r.at[d], (p, t))
        for d, p in enumerate(plane_peers)
    ]
    for c in r_copies + x_copies:
        c.start()
    c_moves[1].start()
    c_moves[0].start()
    xr[i] = x_ref[:, quarter(i)]
    rr[i] = rate_ref[...]

    for w in w_copies:
        w.start()

    def kv_cols(peer):
        return pl.ds(pl.multiple_of(peer * KVHEADS // tp * HEAD, HEAD), HEAD)

    def own_rows(peer):
        return pl.ds(pl.multiple_of(peer * own, own), own)

    swaps = []
    for d, p in enumerate(tp_peers):
        for m, ref in enumerate((k_ref, v_ref)):
            swaps.append(copy(
                ref.at[:, kv_cols(p)], kv.at[s, m, own_rows(t)],
                swap_s.at[m, d], swap_r.at[m, d], (s, p),
            ))
    for c in swaps:
        c.start()
    for m, ref in enumerate((k_ref, v_ref)):
        kv[s, m, own_rows(t), :] = ref[:, kv_cols(t)]

    row_id = lax.broadcasted_iota(jnp.int32, (rows, rows), 0)
    col_id = lax.broadcasted_iota(jnp.int32, (rows, rows), 1)
    causal = row_id >= col_id
    lower = jnp.where(causal, 1.0, 0.0).astype(F32)
    upper = jnp.where(row_id <= col_id, 1.0, 0.0).astype(F32)
    rates = -rate_ref[...]
    cum_t = jnp.dot(rates, upper, precision=PRECISE, preferred_element_type=F32)
    cum = dot_nt(lower, rates, PRECISE)
    from_start = jnp.exp(cum)
    first_half = lax.broadcasted_iota(jnp.int32, (rows, 128), 1) < HDIM

    def pair_cols(value, pair):
        a = value[:, 2 * pair:2 * pair + 1]
        b = value[:, 2 * pair + 1:2 * pair + 2]
        return jnp.where(first_half, a, b)

    for c in swaps:
        c.wait_recv()

    def kv_moves(zz):
        return relay(lambda j: kv.at[zz * PLANE + j], pl_s.at[zz], pl_r.at[zz])

    def up(zz):
        src = kv.at[s]
        return copy(src, src, col_s.at[zz], col_r.at[z], (zz * PLANE + i, t))

    def col_from(zz):
        src = kv.at[zz * PLANE + i]
        return copy(src, src, col_s.at[zz], col_r.at[zz], (s, t))

    @pl.loop(z + 1, planes)
    def _(zz):
        up(zz).start()

    for c in kv_moves(z)[:2]:
        c.start()

    b_moves[1].wait_recv()
    b_moves[2].start()

    for c in r_copies:
        c.wait_recv()
    channel = lax.broadcasted_iota(jnp.int32, (PLANE * heads, span), 1)
    head = (channel + jnp.minimum(i * span, width - span)) // HDIM
    line = lax.broadcasted_iota(jnp.int32, (PLANE * heads, span), 0)
    pick = jnp.concatenate(
        [(line == head + j * heads).astype(F32) for j in range(PLANE)], axis=1
    )
    sums = dot_nt(lower, -jnp.concatenate([rr[j] for j in range(PLANE)], axis=0), PRECISE)
    end = sums[rows - 1:rows, :]
    ends = jnp.broadcast_to(jnp.exp(end), (8, PLANE * heads))
    to_end = jnp.concatenate([jnp.exp(end - sums), ends], axis=0)
    spread = jnp.dot(to_end, pick, precision=PRECISE, preferred_element_type=F32)
    for j in range(PLANE):
        dr[j] = spread[rows:, span * j:span * (j + 1)]
    c_moves[1].wait_recv()
    c_moves[2].start()
    for c in [b_moves[0], b_moves[2]] + x_copies:
        c.wait_recv()
    total = jnp.zeros((bc.shape[3], span), F32)
    decay = jnp.ones((1, span), F32)
    for j in range(PLANE):
        scaled = (xr[j].astype(F32) * spread[:rows, span * j:span * (j + 1)]).astype(BF16)
        block = dot_tn(bc[j, 0], scaled)
        loc[j] = block
        total = dr[j, 0:1, :] * total + block
        decay = decay * dr[j, 0:1, :]
    tot[0] = total
    dr[PLANE] = jnp.broadcast_to(decay, (8, span))

    half = bc.shape[3] // 2
    pieces = [(c, m) for c in range(nch) for m in range(2)]

    def chain(c, m):
        to = (jnp.minimum(z + 1, planes - 1) * PLANE + i, t)
        ms = slice(half * m, half * (m + 1))
        return copy(es.at[c, ms], er.at[c, ms], e_s.at[c, m], e_r.at[c, m], to)

    @pl.when(z == 0)
    def _():
        er[...] = jnp.zeros_like(er)

    @pl.when(z == 0)
    def _():
        for c, m in pieces:
            ms = slice(half * m, half * (m + 1))
            es[c, ms, :] = tot[0, ms, 128 * c:128 * (c + 1)].astype(BF16)
            chain(c, m).start()

    @pl.loop(0, z)
    def _(zz):
        col_from(zz).wait_recv()
        for c in kv_moves(zz)[:2]:
            c.start()

    read_write = dot_nt(c_ref[...], b_ref[...])
    for pair in range(width // 128):
        cc = slice(128 * pair, 128 * (pair + 1))
        factors = []
        for h in (2 * pair, 2 * pair + 1):
            gap = jnp.minimum(cum[:, h:h + 1] - cum_t[h:h + 1, :], 0.0)
            factors.append(jnp.where(causal, jnp.exp(gap) * read_write, 0.0).astype(BF16))
        x = x_ref[:, cc]
        zero = jnp.zeros_like(x)
        stacked = jnp.concatenate(
            [jnp.where(first_half, x, zero), jnp.where(first_half, zero, x)], axis=0
        )
        yacc[:, cc] = dot(jnp.concatenate(factors, axis=1), stacked)
        grow[:, cc] = pair_cols(from_start, pair)

    @pl.loop(0, z + 1)
    def _(zz):
        moves = kv_moves(zz)
        moves[1].wait_recv()
        moves[2].start()

    for h in range(nq):
        lo = pl.multiple_of((t * nq + h) * HEAD, HEAD)
        qs[h * rows:(h + 1) * rows, :] = q_ref[:, pl.ds(lo, HEAD)]
    stack = nq * rows
    acc[...] = jnp.zeros_like(acc)
    norm[...] = jnp.zeros_like(norm)
    peak[...] = jnp.full_like(peak, -1e30)
    scale = 1.0 / math.sqrt(HEAD)
    wide = PLANE * rows

    def attend(zz):
        moves = kv_moves(zz)
        moves[0].wait_recv()
        moves[2].wait_recv()
        keys = kv[pl.ds(zz * PLANE, PLANE), 0].reshape(wide, HEAD)
        vals = kv[pl.ds(zz * PLANE, PLANE), 1].reshape(wide, HEAD)
        for h in range(nq):
            hh = slice(h * rows, (h + 1) * rows)
            scores = dot_nt(qs[hh, :], keys) * scale
            key_id = lax.broadcasted_iota(jnp.int32, (rows, wide), 1)
            query_id = lax.broadcasted_iota(jnp.int32, (rows, wide), 0)
            ahead = (z - zz) * wide + i * rows
            scores = jnp.where(key_id <= query_id + ahead, scores, -1e30)
            old = peak[hh, 0:1]
            new = jnp.maximum(old, jnp.max(scores, axis=1, keepdims=True))
            weights = jnp.exp(scores - new)
            shrink = jnp.exp(old - new)
            norm[hh, 0:1] = norm[hh, 0:1] * shrink + jnp.sum(weights, axis=1, keepdims=True)
            acc[hh, :] = acc[hh, :] * shrink + dot(weights.astype(BF16), vals)
            peak[hh, 0:1] = new

    early = z // 2 + (z // (planes - 1)) * (z + 1 - z // 2)

    @pl.loop(0, early)
    def _(zz):
        attend(zz)

    c_moves[0].wait_recv()
    c_moves[2].wait_recv()
    y_copies = []

    @pl.when((z > 0) & (z < planes - 1))
    def _():
        for c, m in pieces:
            cc = slice(128 * c, 128 * (c + 1))
            ms = slice(half * m, half * (m + 1))
            chain(c, m).wait_recv()
            entering = er[c, ms, :].astype(F32)
            es[c, ms, :] = (dr[PLANE, 0:1, cc] * entering + tot[0, ms, cc]).astype(BF16)
            chain(c, m).start()

    for c in range(nch):
        cc = slice(128 * c, 128 * (c + 1))

        @pl.when((z > 0) & (z == planes - 1))
        def _():
            for m in range(2):
                chain(c, m).wait_recv()

        state = er[c].astype(F32)
        for j in range(PLANE):
            ysend[c, j] = dot(bc[j, 1], state.astype(BF16)).astype(BF16)
            if j < PLANE - 1:
                state = dr[j, 0:1, cc] * state + loc[j, :, cc]
        sends = [
            copy(ysend.at[c, plane_index[d]], yrecv.at[c, i], y_s.at[c, d], y_r.at[c, d], (p, t))
            for d, p in enumerate(plane_peers)
        ]
        for m in sends:
            m.start()
        y_copies.append(sends)
        yrecv[c, i] = ysend[c, i]

    @pl.loop(early, z + 1)
    def _(zz):
        attend(zz)

    for h in range(nq):
        hh = slice(h * rows, (h + 1) * rows)
        attn[:, h * HEAD:(h + 1) * HEAD] = (acc[hh, :] / norm[hh, 0:1]).astype(BF16)
    for w in w_copies:
        w.wait()
    for k in range(ncol):
        cc = slice(k * cols, (k + 1) * cols)
        part[:, cc] = dot(attn[...], wa[:, cc])

    p_copies = []
    done = 0
    for step in range(nch):
        for m in y_copies[step]:
            m.wait_recv()
        depth = 128 * len(tiles[step])
        for k, (q, lo) in enumerate(tiles[step]):
            cc = slice(lo, lo + 128)
            g = gate_ref[:, cc].astype(F32)
            raw = yacc[:, cc] + grow[:, cc] * yrecv[step, q].astype(F32)
            at = done + 128 * k
            ssm[:, at:at + 128] = (raw * (g / (1.0 + jnp.exp(-g)))).astype(BF16)
        for k in range(ncol):
            cc = slice(k * cols, (k + 1) * cols)
            value = part[:, cc] + dot(ssm[:, done:done + depth], ws[done:done + depth, cc])
            part[:, cc] = value
            if step == nch - 1:
                psend[k] = value.astype(BF16)
                for d, p in enumerate(tp_peers):
                    c = copy(
                        psend.at[k, own_rows(p)], precv.at[d, :, k * cols:(k + 1) * cols],
                        p_s.at[d, k], p_r.at[d, k], (s, p),
                    )
                    c.start()
                    p_copies.append((d, k, c))
        done += depth
    keep = pltpu.make_async_copy(part.at[own_rows(t)], out_ref, o_s)
    keep.start()
    for _, _, c in p_copies:
        c.wait_recv()
    keep.wait()

    moved = swaps + b_moves + c_moves + r_copies + x_copies + sum(y_copies, [])
    for c in moved + [c for _, _, c in p_copies]:
        c.wait_send()

    @pl.loop(z + 1, planes)
    def _(zz):
        up(zz).wait_send()

    @pl.loop(0, z + 1)
    def _(zz):
        for c in kv_moves(zz):
            c.wait_send()

    @pl.when(z < planes - 1)
    def _():
        for c, m in pieces:
            chain(c, m).wait_send()


def add_shares(mine_ref, others_ref, out_ref):
    total = mine_ref[...]
    for d in range(others_ref.shape[0]):
        total = total + others_ref[d].astype(F32)
    out_ref[...] = total


def local(
    n, tp,
    queries, key_rows, value_rows, ssm_input, gate_input, write_vectors, read_vectors,
    decay_rates, attn_out_weight, ssm_out_weight,
):
    rows = queries.shape[0]
    width = ssm_input.shape[1]
    heads = decay_rates.shape[1]
    state = write_vectors.shape[1]
    model = attn_out_weight.shape[1]
    nq = queries.shape[1] // HEAD // tp
    planes = n // PLANE
    own = rows // tp
    span, _ = quarter_starts(width)
    nch = span // 128
    ncol = 8
    cols = model // ncol
    peers = PLANE - 1
    vmem = pltpu.VMEM
    dma = pltpu.SemaphoreType.DMA
    mine, others = pl.pallas_call(
        functools.partial(kernel, n, tp, heads, nq),
        out_shape=(
            jax.ShapeDtypeStruct((own, model), F32),
            jax.ShapeDtypeStruct((tp - 1, own, model), BF16),
        ),
        in_specs=[pl.BlockSpec(memory_space=pl.ANY)] * 10,
        out_specs=(pl.BlockSpec(memory_space=pl.ANY),) * 2,
        scratch_shapes=[
            vmem(queries.shape, BF16),
            vmem(key_rows.shape, BF16),
            vmem(value_rows.shape, BF16),
            vmem(ssm_input.shape, BF16),
            vmem(gate_input.shape, BF16),
            vmem(write_vectors.shape, BF16),
            vmem(read_vectors.shape, BF16),
            vmem((heads, rows), F32),
            vmem(attn_out_weight.shape, BF16),
            vmem(ssm_out_weight.shape, BF16),
            vmem((n, 2, rows, HEAD), BF16),
            vmem((PLANE, 2, rows, state), BF16),
            vmem((PLANE, rows, span), BF16),
            vmem((PLANE, heads, rows), F32),
            vmem((PLANE + 1, 8, span), F32),
            vmem((PLANE, state, span), F32),
            vmem((1, state, span), F32),
            vmem((nch, state, 128), BF16),
            vmem((nch, state, 128), BF16),
            vmem((nch, PLANE, rows, 128), BF16),
            vmem((nch, PLANE, rows, 128), BF16),
            vmem((ncol, rows, cols), BF16),
            vmem((nq * rows, HEAD), BF16),
            vmem((rows, nq * HEAD), BF16),
            vmem((rows, width), F32),
            vmem((rows, width), F32),
            vmem((rows, model), F32),
            vmem((rows, width), BF16),
            vmem((nq * rows, HEAD), F32),
            vmem((nq * rows, HEAD), F32),
            vmem((nq * rows, HEAD), F32),
            dma((width // 128 + 1,)),
            dma((2, tp - 1)),
            dma((2, tp - 1)),
            dma((planes,)),
            dma((planes,)),
            dma((planes, peers)),
            dma((planes, peers)),
            dma((2, peers)),
            dma((2, peers)),
            dma((peers,)),
            dma((peers,)),
            dma((peers,)),
            dma((peers,)),
            dma((nch, 2)),
            dma((nch, 2)),
            dma((nch, peers)),
            dma((nch, peers)),
            dma((tp - 1, ncol)),
            dma((tp - 1, ncol)),
            dma,
            dma((8,)),
        ],
        compiler_params=pltpu.CompilerParams(
            collective_id=0, has_side_effects=True, vmem_limit_bytes=56 * 1024 * 1024
        ),
    )(
        queries, key_rows, value_rows, ssm_input, gate_input, write_vectors, read_vectors,
        decay_rates.T, attn_out_weight, ssm_out_weight,
    )
    return pl.pallas_call(
        add_shares,
        out_shape=jax.ShapeDtypeStruct((own, model), F32),
        in_specs=[pl.BlockSpec(memory_space=pltpu.VMEM)] * 2,
        out_specs=pl.BlockSpec(memory_space=pltpu.VMEM),
    )(mine, others)


def solution(mesh):
    placed = (
        P("seq", None),
        P(("seq", "tp"), None),
        P(("seq", "tp"), None),
        P("seq", "tp"),
        P("seq", "tp"),
        P("seq", None),
        P("seq", None),
        P("seq", "tp"),
        P("tp", None),
        P("tp", None),
    )
    body = functools.partial(local, mesh.shape["seq"], mesh.shape["tp"])
    return jax.shard_map(
        body, mesh=mesh, in_specs=placed, out_specs=P(("seq", "tp"), None), check_vma=False
    )
```

```python
import functools
import math

import jax
import jax.numpy as jnp
from jax import lax
from jax.experimental import pallas as pl
from jax.experimental.pallas import tpu as pltpu
from jax.sharding import PartitionSpec as P

KVHEADS = 2
HEAD = 128
HDIM = 64
PLANE = 4
MESH = pl.DeviceIdType.MESH
F32 = jnp.float32
BF16 = jnp.bfloat16
PRECISE = lax.Precision.HIGHEST


def dot(a, b):
    return jnp.dot(a, b, preferred_element_type=F32)


def dot_tn(a, b, precision=None):
    dims = (((0,), (0,)), ((), ()))
    return lax.dot_general(a, b, dims, precision=precision, preferred_element_type=F32)


def dot_nt(a, b, precision=None):
    dims = (((1,), (1,)), ((), ()))
    return lax.dot_general(a, b, dims, precision=precision, preferred_element_type=F32)


def quarter_starts(width):
    span = -(-width // (PLANE * 128)) * 128
    return span, [min(q * span, width - span) for q in range(PLANE)]


def kernel(
    n, tp, heads, nq,
    q_in, k_in, v_in, x_in, gate_in, b_in, c_in, rate_in, wa_hbm, ws_hbm,
    out_ref, precv,
    q_ref, k_ref, v_ref, x_ref, gate_ref, b_ref, c_ref, rate_ref,
    wa, ws, kv, bc, xr, rr, dr, loc, tot, er, es, ysend, yrecv, psend,
    qs, attn, yacc, grow, part, ssm, acc, peak, norm,
    wsem, swap_s, swap_r, col_s, col_r, pl_s, pl_r, bc_s, bc_r, x_s, x_r, d_s, d_r,
    e_s, e_r, y_s, y_r, p_s, p_r, o_s, in_s,
):
    s = lax.axis_index("seq")
    t = lax.axis_index("tp")
    planes = n // PLANE
    z = s // PLANE
    i = s % PLANE
    rows = q_ref.shape[0]
    width = x_ref.shape[1]
    model = wa.shape[1]
    own = rows // tp
    span, starts = quarter_starts(width)
    nch = span // 128
    ncol = psend.shape[0]
    cols = model // ncol

    def copy(src, dst, send, recv, to):
        return pltpu.make_async_remote_copy(
            src_ref=src, dst_ref=dst, send_sem=send, recv_sem=recv,
            device_id=to, device_id_type=MESH,
        )

    tiles = []
    for c in range(nch):
        seen = [lo for step in tiles for _, lo in step]
        step = []
        for q in range(PLANE):
            lo = starts[q] + 128 * c
            if lo not in seen:
                step.append((q, lo))
                seen.append(lo)
        tiles.append(step)
    order = [lo for step in tiles for _, lo in step]
    w_copies = [pltpu.make_async_copy(wa_hbm, wa, wsem.at[len(order)])] + [
        pltpu.make_async_copy(
            ws_hbm.at[pl.ds(lo, 128)], ws.at[pl.ds(128 * k, 128)], wsem.at[k]
        )
        for k, lo in enumerate(order)
    ]
    fetch = [
        pltpu.make_async_copy(src, dst, in_s.at[k])
        for k, (src, dst) in enumerate((
            (b_in, b_ref), (rate_in, rate_ref), (x_in, x_ref), (c_in, c_ref),
            (k_in, k_ref), (v_in, v_ref), (q_in, q_ref), (gate_in, gate_ref),
        ))
    ]
    for c in fetch:
        c.start()

    sib = i + 1 - 2 * (i % 2)
    ynb = (i + 2) % PLANE
    dia = (sib + 2) % PLANE
    plane_index = [ynb, dia, sib]
    plane_peers = [z * PLANE + j for j in plane_index]
    tp_peers = [(t + d) % tp for d in range(1, tp)]
    col_peers = [((z + d) % planes) * PLANE + i for d in range(1, planes)]

    barrier = pltpu.get_barrier_semaphore()
    for p in plane_peers + col_peers:
        pl.semaphore_signal(barrier, inc=1, device_id=(p, t), device_id_type=MESH)
    for p in tp_peers:
        pl.semaphore_signal(barrier, inc=1, device_id=(s, p), device_id_type=MESH)
    for c in fetch:
        c.wait()
    pl.semaphore_wait(barrier, len(plane_peers) + len(col_peers) + len(tp_peers))

    def relay(ref_of, send, recv):
        def move(block, kind, to):
            ref = ref_of(block)
            return copy(ref, ref, send.at[kind], recv.at[kind], (z * PLANE + to, t))
        return [move(i, 0, sib), move(i, 1, ynb), move(ynb, 2, sib)]

    bc[i, 0] = b_ref[...]
    bc[i, 1] = c_ref[...]
    b_moves = relay(lambda j: bc.at[j, 0], bc_s.at[0], bc_r.at[0])
    c_moves = relay(lambda j: bc.at[j, 1], bc_s.at[1], bc_r.at[1])
    b_moves[1].start()
    b_moves[0].start()

    def quarter(q):
        return pl.ds(pl.multiple_of(jnp.minimum(q * span, width - span), 128), span)

    r_copies = [
        copy(rate_ref, rr.at[i], d_s.at[d], d_r.at[d], (p, t))
        for d, p in enumerate(plane_peers)
    ]
    x_copies = [
        copy(x_ref.at[:, quarter(plane_index[d])], xr.at[i], x_s.at[d], x_r.at[d], (p, t))
        for d, p in enumerate(plane_peers)
    ]
    for c in r_copies + x_copies:
        c.start()
    c_moves[1].start()
    c_moves[0].start()
    xr[i] = x_ref[:, quarter(i)]
    rr[i] = rate_ref[...]

    for w in w_copies:
        w.start()

    def kv_cols(peer):
        return pl.ds(pl.multiple_of(peer * KVHEADS // tp * HEAD, HEAD), HEAD)

    def own_rows(peer):
        return pl.ds(pl.multiple_of(peer * own, own), own)

    swaps = []
    for d, p in enumerate(tp_peers):
        for m, ref in enumerate((k_ref, v_ref)):
            swaps.append(copy(
                ref.at[:, kv_cols(p)], kv.at[s, m, own_rows(t)],
                swap_s.at[m, d], swap_r.at[m, d], (s, p),
            ))
    for c in swaps:
        c.start()
    for m, ref in enumerate((k_ref, v_ref)):
        kv[s, m, own_rows(t), :] = ref[:, kv_cols(t)]

    row_id = lax.broadcasted_iota(jnp.int32, (rows, rows), 0)
    col_id = lax.broadcasted_iota(jnp.int32, (rows, rows), 1)
    causal = row_id >= col_id
    lower = jnp.where(causal, 1.0, 0.0).astype(F32)
    upper = jnp.where(row_id <= col_id, 1.0, 0.0).astype(F32)
    rates = -rate_ref[...]
    cum_t = jnp.dot(rates, upper, precision=PRECISE, preferred_element_type=F32)
    cum = dot_nt(lower, rates, PRECISE)
    from_start = jnp.exp(cum)
    first_half = lax.broadcasted_iota(jnp.int32, (rows, 128), 1) < HDIM

    def pair_cols(value, pair):
        a = value[:, 2 * pair:2 * pair + 1]
        b = value[:, 2 * pair + 1:2 * pair + 2]
        return jnp.where(first_half, a, b)

    for c in swaps:
        c.wait_recv()

    def kv_moves(zz):
        return relay(lambda j: kv.at[zz * PLANE + j], pl_s.at[zz], pl_r.at[zz])

    def up(zz):
        src = kv.at[s]
        return copy(src, src, col_s.at[zz], col_r.at[z], (zz * PLANE + i, t))

    def col_from(zz):
        src = kv.at[zz * PLANE + i]
        return copy(src, src, col_s.at[zz], col_r.at[zz], (s, t))

    @pl.loop(z + 1, planes)
    def _(zz):
        up(zz).start()

    for c in kv_moves(z)[:2]:
        c.start()

    b_moves[1].wait_recv()
    b_moves[2].start()

    for c in r_copies:
        c.wait_recv()
    channel = lax.broadcasted_iota(jnp.int32, (PLANE * heads, span), 1)
    head = (channel + jnp.minimum(i * span, width - span)) // HDIM
    line = lax.broadcasted_iota(jnp.int32, (PLANE * heads, span), 0)
    pick = jnp.concatenate(
        [(line == head + j * heads).astype(F32) for j in range(PLANE)], axis=1
    )
    sums = dot_nt(lower, -jnp.concatenate([rr[j] for j in range(PLANE)], axis=0), PRECISE)
    end = sums[rows - 1:rows, :]
    ends = jnp.broadcast_to(jnp.exp(end), (8, PLANE * heads))
    to_end = jnp.concatenate([jnp.exp(end - sums), ends], axis=0)
    spread = jnp.dot(to_end, pick, precision=PRECISE, preferred_element_type=F32)
    for j in range(PLANE):
        dr[j] = spread[rows:, span * j:span * (j + 1)]
    c_moves[1].wait_recv()
    c_moves[2].start()
    for c in [b_moves[0], b_moves[2]] + x_copies:
        c.wait_recv()
    total = jnp.zeros((bc.shape[3], span), F32)
    decay = jnp.ones((1, span), F32)
    for j in range(PLANE):
        scaled = (xr[j].astype(F32) * spread[:rows, span * j:span * (j + 1)]).astype(BF16)
        block = dot_tn(bc[j, 0], scaled)
        loc[j] = block
        total = dr[j, 0:1, :] * total + block
        decay = decay * dr[j, 0:1, :]
    tot[0] = total
    dr[PLANE] = jnp.broadcast_to(decay, (8, span))

    half = bc.shape[3] // 2
    pieces = [(c, m) for c in range(nch) for m in range(2)]

    def chain(c, m):
        to = (jnp.minimum(z + 1, planes - 1) * PLANE + i, t)
        ms = slice(half * m, half * (m + 1))
        return copy(es.at[c, ms], er.at[c, ms], e_s.at[c, m], e_r.at[c, m], to)

    @pl.when(z == 0)
    def _():
        er[...] = jnp.zeros_like(er)

    @pl.when(z == 0)
    def _():
        for c, m in pieces:
            ms = slice(half * m, half * (m + 1))
            es[c, ms, :] = tot[0, ms, 128 * c:128 * (c + 1)].astype(BF16)
            chain(c, m).start()

    @pl.loop(0, z)
    def _(zz):
        col_from(zz).wait_recv()
        for c in kv_moves(zz)[:2]:
            c.start()

    read_write = dot_nt(c_ref[...], b_ref[...])
    for pair in range(width // 128):
        cc = slice(128 * pair, 128 * (pair + 1))
        factors = []
        for h in (2 * pair, 2 * pair + 1):
            gap = jnp.minimum(cum[:, h:h + 1] - cum_t[h:h + 1, :], 0.0)
            factors.append(jnp.where(causal, jnp.exp(gap) * read_write, 0.0).astype(BF16))
        x = x_ref[:, cc]
        zero = jnp.zeros_like(x)
        stacked = jnp.concatenate(
            [jnp.where(first_half, x, zero), jnp.where(first_half, zero, x)], axis=0
        )
        yacc[:, cc] = dot(jnp.concatenate(factors, axis=1), stacked)
        grow[:, cc] = pair_cols(from_start, pair)

    @pl.loop(0, z + 1)
    def _(zz):
        moves = kv_moves(zz)
        moves[1].wait_recv()
        moves[2].start()

    for h in range(nq):
        lo = pl.multiple_of((t * nq + h) * HEAD, HEAD)
        qs[h * rows:(h + 1) * rows, :] = q_ref[:, pl.ds(lo, HEAD)]
    stack = nq * rows
    acc[...] = jnp.zeros_like(acc)
    norm[...] = jnp.zeros_like(norm)
    peak[...] = jnp.full_like(peak, -1e30)
    scale = 1.0 / math.sqrt(HEAD)
    wide = PLANE * rows

    def attend(zz, masked):
        moves = kv_moves(zz)
        moves[0].wait_recv()
        moves[2].wait_recv()
        keys = kv[pl.ds(zz * PLANE, PLANE), 0].reshape(wide, HEAD)
        vals = kv[pl.ds(zz * PLANE, PLANE), 1].reshape(wide, HEAD)
        for h in range(nq):
            hh = slice(h * rows, (h + 1) * rows)
            scores = dot_nt(qs[hh, :], keys) * scale
            if masked:
                key_id = lax.broadcasted_iota(jnp.int32, (rows, wide), 1)
                query_id = lax.broadcasted_iota(jnp.int32, (rows, wide), 0) + i * rows
                scores = jnp.where(key_id <= query_id, scores, -1e30)
            old = peak[hh, 0:1]
            new = jnp.maximum(old, jnp.max(scores, axis=1, keepdims=True))
            weights = jnp.exp(scores - new)
            shrink = jnp.exp(old - new)
            norm[hh, 0:1] = norm[hh, 0:1] * shrink + jnp.sum(weights, axis=1, keepdims=True)
            acc[hh, :] = acc[hh, :] * shrink + dot(weights.astype(BF16), vals)
            peak[hh, 0:1] = new

    early = z // 2

    @pl.loop(0, early)
    def _(zz):
        attend(zz, False)

    c_moves[0].wait_recv()
    c_moves[2].wait_recv()
    y_copies = []

    @pl.when((z > 0) & (z < planes - 1))
    def _():
        for c, m in pieces:
            cc = slice(128 * c, 128 * (c + 1))
            ms = slice(half * m, half * (m + 1))
            chain(c, m).wait_recv()
            entering = er[c, ms, :].astype(F32)
            es[c, ms, :] = (dr[PLANE, 0:1, cc] * entering + tot[0, ms, cc]).astype(BF16)
            chain(c, m).start()

    for c in range(nch):
        cc = slice(128 * c, 128 * (c + 1))

        @pl.when((z > 0) & (z == planes - 1))
        def _():
            for m in range(2):
                chain(c, m).wait_recv()

        state = er[c].astype(F32)
        for j in range(PLANE):
            ysend[c, j] = dot(bc[j, 1], state.astype(BF16)).astype(BF16)
            if j < PLANE - 1:
                state = dr[j, 0:1, cc] * state + loc[j, :, cc]
        sends = [
            copy(ysend.at[c, plane_index[d]], yrecv.at[c, i], y_s.at[c, d], y_r.at[c, d], (p, t))
            for d, p in enumerate(plane_peers)
        ]
        for m in sends:
            m.start()
        y_copies.append(sends)
        yrecv[c, i] = ysend[c, i]

    attend(z, True)

    @pl.loop(early, z)
    def _(zz):
        attend(zz, False)

    for h in range(nq):
        hh = slice(h * rows, (h + 1) * rows)
        attn[:, h * HEAD:(h + 1) * HEAD] = (acc[hh, :] / norm[hh, 0:1]).astype(BF16)
    for w in w_copies:
        w.wait()
    for k in range(ncol):
        cc = slice(k * cols, (k + 1) * cols)
        part[:, cc] = dot(attn[...], wa[:, cc])

    p_copies = []
    done = 0
    for step in range(nch):
        for m in y_copies[step]:
            m.wait_recv()
        depth = 128 * len(tiles[step])
        for k, (q, lo) in enumerate(tiles[step]):
            cc = slice(lo, lo + 128)
            g = gate_ref[:, cc].astype(F32)
            raw = yacc[:, cc] + grow[:, cc] * yrecv[step, q].astype(F32)
            at = done + 128 * k
            ssm[:, at:at + 128] = (raw * (g / (1.0 + jnp.exp(-g)))).astype(BF16)
        for k in range(ncol):
            cc = slice(k * cols, (k + 1) * cols)
            value = part[:, cc] + dot(ssm[:, done:done + depth], ws[done:done + depth, cc])
            part[:, cc] = value
            if step == nch - 1:
                psend[k] = value.astype(BF16)
                for d, p in enumerate(tp_peers):
                    c = copy(
                        psend.at[k, own_rows(p)], precv.at[d, :, k * cols:(k + 1) * cols],
                        p_s.at[d, k], p_r.at[d, k], (s, p),
                    )
                    c.start()
                    p_copies.append((d, k, c))
        done += depth
    keep = pltpu.make_async_copy(part.at[own_rows(t)], out_ref, o_s)
    keep.start()
    for _, _, c in p_copies:
        c.wait_recv()
    keep.wait()

    moved = swaps + b_moves + c_moves + r_copies + x_copies + sum(y_copies, [])
    for c in moved + [c for _, _, c in p_copies]:
        c.wait_send()

    @pl.loop(z + 1, planes)
    def _(zz):
        up(zz).wait_send()

    @pl.loop(0, z + 1)
    def _(zz):
        for c in kv_moves(zz):
            c.wait_send()

    @pl.when(z < planes - 1)
    def _():
        for c, m in pieces:
            chain(c, m).wait_send()


def add_shares(mine_ref, others_ref, out_ref):
    total = mine_ref[...]
    for d in range(others_ref.shape[0]):
        total = total + others_ref[d].astype(F32)
    out_ref[...] = total


def local(
    n, tp,
    queries, key_rows, value_rows, ssm_input, gate_input, write_vectors, read_vectors,
    decay_rates, attn_out_weight, ssm_out_weight,
):
    rows = queries.shape[0]
    width = ssm_input.shape[1]
    heads = decay_rates.shape[1]
    state = write_vectors.shape[1]
    model = attn_out_weight.shape[1]
    nq = queries.shape[1] // HEAD // tp
    planes = n // PLANE
    own = rows // tp
    span, _ = quarter_starts(width)
    nch = span // 128
    ncol = 8
    cols = model // ncol
    peers = PLANE - 1
    vmem = pltpu.VMEM
    dma = pltpu.SemaphoreType.DMA
    mine, others = pl.pallas_call(
        functools.partial(kernel, n, tp, heads, nq),
        out_shape=(
            jax.ShapeDtypeStruct((own, model), F32),
            jax.ShapeDtypeStruct((tp - 1, own, model), BF16),
        ),
        in_specs=[pl.BlockSpec(memory_space=pl.ANY)] * 10,
        out_specs=(pl.BlockSpec(memory_space=pl.ANY),) * 2,
        scratch_shapes=[
            vmem(queries.shape, BF16),
            vmem(key_rows.shape, BF16),
            vmem(value_rows.shape, BF16),
            vmem(ssm_input.shape, BF16),
            vmem(gate_input.shape, BF16),
            vmem(write_vectors.shape, BF16),
            vmem(read_vectors.shape, BF16),
            vmem((heads, rows), F32),
            vmem(attn_out_weight.shape, BF16),
            vmem(ssm_out_weight.shape, BF16),
            vmem((n, 2, rows, HEAD), BF16),
            vmem((PLANE, 2, rows, state), BF16),
            vmem((PLANE, rows, span), BF16),
            vmem((PLANE, heads, rows), F32),
            vmem((PLANE + 1, 8, span), F32),
            vmem((PLANE, state, span), F32),
            vmem((1, state, span), F32),
            vmem((nch, state, 128), BF16),
            vmem((nch, state, 128), BF16),
            vmem((nch, PLANE, rows, 128), BF16),
            vmem((nch, PLANE, rows, 128), BF16),
            vmem((ncol, rows, cols), BF16),
            vmem((nq * rows, HEAD), BF16),
            vmem((rows, nq * HEAD), BF16),
            vmem((rows, width), F32),
            vmem((rows, width), F32),
            vmem((rows, model), F32),
            vmem((rows, width), BF16),
            vmem((nq * rows, HEAD), F32),
            vmem((nq * rows, HEAD), F32),
            vmem((nq * rows, HEAD), F32),
            dma((width // 128 + 1,)),
            dma((2, tp - 1)),
            dma((2, tp - 1)),
            dma((planes,)),
            dma((planes,)),
            dma((planes, peers)),
            dma((planes, peers)),
            dma((2, peers)),
            dma((2, peers)),
            dma((peers,)),
            dma((peers,)),
            dma((peers,)),
            dma((peers,)),
            dma((nch, 2)),
            dma((nch, 2)),
            dma((nch, peers)),
            dma((nch, peers)),
            dma((tp - 1, ncol)),
            dma((tp - 1, ncol)),
            dma,
            dma((8,)),
        ],
        compiler_params=pltpu.CompilerParams(
            collective_id=0, has_side_effects=True, vmem_limit_bytes=56 * 1024 * 1024
        ),
    )(
        queries, key_rows, value_rows, ssm_input, gate_input, write_vectors, read_vectors,
        decay_rates.T, attn_out_weight, ssm_out_weight,
    )
    return pl.pallas_call(
        add_shares,
        out_shape=jax.ShapeDtypeStruct((own, model), F32),
        in_specs=[pl.BlockSpec(memory_space=pltpu.VMEM)] * 2,
        out_specs=pl.BlockSpec(memory_space=pltpu.VMEM),
    )(mine, others)


def solution(mesh):
    placed = (
        P("seq", None),
        P(("seq", "tp"), None),
        P(("seq", "tp"), None),
        P("seq", "tp"),
        P("seq", "tp"),
        P("seq", None),
        P("seq", None),
        P("seq", "tp"),
        P("tp", None),
        P("tp", None),
    )
    body = functools.partial(local, mesh.shape["seq"], mesh.shape["tp"])
    return jax.shard_map(
        body, mesh=mesh, in_specs=placed, out_specs=P(("seq", "tp"), None), check_vma=False
    )
```
